512 devices in a mesh: ctx: 16 (over y, z_lo), kvh: 8 (over x, core), rep: 4 (over z_hi).
Axes of the slice: x: 4, y: 8, z: 8 (z_hi: 4, z_lo: 2; z = z_hi * 2 + z_lo), core: 2. Of those that a mesh axis runs over, the one named last changes fastest.
Arguments:
- queries: bfloat16 [256, 128, 128], P(('ctx', 'rep'), 'kvh'), may hold values from -5 to 5
- prompt_keys: bfloat16 [65536, 8, 128], P('ctx', 'kvh'), may hold values from -5 to 5
- prompt_values: bfloat16 [65536, 8, 128], P('ctx', 'kvh'), may hold values from -2.5 to 2.5
- suffix_keys: bfloat16 [256, 512, 8, 128], P(('ctx', 'rep'), None, 'kvh'), may hold values from -10 to 10
- suffix_values: bfloat16 [256, 512, 8, 128], P(('ctx', 'rep'), None, 'kvh'), may hold values from -2.5 to 2.5
- suffix_len: int32 [256], P(('ctx', 'rep')), may hold values from 0 to 512, as said below
- out_weight: bfloat16 [16384, 16384], P('kvh', ('ctx', 'rep')), may hold values from -0.046875 to 0.046875
Outputs:
- attended: bfloat16 [256, 128, 128], P(('ctx', 'rep'), 'kvh')
- projected: bfloat16 [256, 16384], P('kvh', ('ctx', 'rep'))
The draws below stay inside these ranges and needn't reach their ends.
Inputs may be any that keep to these rules, and one draw needn't show every extreme that they name: `suffix_len`: some continuation has 512 live private positions and some has none.
All inputs are finite; a program needn't handle non-finite values.
Results may differ from the reference program's by a relative error of at most 0.015.
Values may be sent and summed in bfloat16 or wider, within the bound.
No kernel may reach another device: no remote copies, remote signals or barrier semaphores. Data moves between devices by JAX's collectives and lax.ppermute only.
A program may use at most 64 MiB of HBM per device.

```python
import math
import jax
import jax.numpy as jnp
from jax import lax

D = 16384
QPK = 16
HD = 128
CONT_DEV = 4
SUF = 512
KV_HEADS = 8
HEADS = 128
PROMPT = 65536
CONT = 256


def draw_queries(key, part):
    key = jax.random.fold_in(key, 3)
    values = jnp.clip(1.7 * jax.random.normal(key, (CONT, HEADS, HD), jnp.float32), -5.0, 5.0)
    return values.astype(jnp.bfloat16)


def draw_prompt_keys(key, part):
    key = jax.random.fold_in(key, 5)
    values = jnp.clip(1.7 * jax.random.normal(key, (PROMPT, KV_HEADS, HD), jnp.float32), -5.0, 5.0)
    return values.astype(jnp.bfloat16)


def draw_suffix_len(key, part):
    key = jax.random.fold_in(key, 7)
    lengths = jax.random.randint(jax.random.fold_in(key, 1), (CONT,), 0, SUF + 1)
    longest = jax.random.randint(jax.random.fold_in(key, 2), (), 0, CONT)
    positions = jnp.arange(CONT, dtype=jnp.int32)
    lengths = jnp.where(positions == longest, SUF, lengths)
    lengths = jnp.where(positions == (longest + 1) % CONT, 0, lengths)
    return lengths.astype(jnp.int32)


def block_scale(own_key, dims, shards, least, high):
    def one(axis_at, parts):
        heights = jax.random.uniform(jax.random.fold_in(jax.random.fold_in(own_key, 6), axis_at), (parts,), jnp.float32, least / len(shards), high / len(shards))
        return jnp.repeat(jnp.exp(heights), dims[axis_at] // parts).reshape((-1,) + (1,) * (len(dims) - axis_at - 1))

    loudness = one(*shards[0])
    for cut in shards[1:]:
        loudness = loudness * one(*cut)
    return loudness


def scatter_about(key, dims, scale, limit, shards=(), kind=jnp.bfloat16):
    drawn = jax.random.normal(key, dims, jnp.float32) * scale
    if len(shards) > 0:
        drawn = block_scale(key, dims, shards, -0.22, 0.18) * drawn
    return jnp.clip(drawn, min=-limit, max=limit).astype(kind)


def setup_inputs(seed: int = 0) -> dict:
    key_list = jax.random.split(jax.random.key(seed), 8)
    queries = draw_queries(jax.random.fold_in(key_list[7], 71), 0)
    prompt_keys = draw_prompt_keys(jax.random.fold_in(key_list[7], 71), 0)
    prompt_values = scatter_about(key_list[2], (PROMPT, KV_HEADS, HD), 0.5, 2.5, ((0, 16), (1, 8)))
    suffix_keys = scatter_about(key_list[3], (CONT, SUF, KV_HEADS, HD), 2.4, 10.0, ((0, 64), (2, 8)))
    suffix_values = scatter_about(key_list[4], (CONT, SUF, KV_HEADS, HD), 0.5, 2.5, ((0, 64), (2, 8)))
    suffix_len = draw_suffix_len(jax.random.fold_in(key_list[7], 71), 0)
    out_weight = scatter_about(key_list[6], (HEADS * HD, D), (HEADS * HD) ** -0.5, 0.046875, ((0, 8), (1, 64)))
    return {"queries": queries, "prompt_keys": prompt_keys, "prompt_values": prompt_values, "suffix_keys": suffix_keys, "suffix_values": suffix_values, "suffix_len": suffix_len, "out_weight": out_weight}


FAR_BELOW = -1e+30

def reference(queries, prompt_keys, prompt_values, suffix_keys, suffix_values, suffix_len, out_weight):
    factor = 1.0 / math.sqrt(HD)
    block_ids = jnp.arange(CONT // CONT_DEV, dtype=jnp.int32)
    group_ids = jnp.arange(KV_HEADS, dtype=jnp.int32)

    def group_attention(group):
        key_block = lax.dynamic_index_in_dim(prompt_keys, group, 1, keepdims=False)
        value_block = lax.dynamic_index_in_dim(prompt_values, group, 1, keepdims=False)

        def block_attention(block):
            first_row = (block * CONT_DEV).astype(jnp.int32)
            query_slab = lax.dynamic_slice_in_dim(lax.dynamic_slice_in_dim(queries, first_row, CONT_DEV, 0), (group * QPK).astype(jnp.int32), QPK, 1)
            suffix_key_set = lax.dynamic_index_in_dim(lax.dynamic_slice_in_dim(suffix_keys, first_row, CONT_DEV, 0), group, 2, keepdims=False)
            suffix_value_set = lax.dynamic_index_in_dim(lax.dynamic_slice_in_dim(suffix_values, first_row, CONT_DEV, 0), group, 2, keepdims=False)
            lengths = lax.dynamic_slice_in_dim(suffix_len, first_row, CONT_DEV, 0)
            query_flat = query_slab.reshape(CONT_DEV * QPK, HD)
            prompt_scores = jnp.dot(query_flat, key_block.T, preferred_element_type=jnp.float32) * factor
            suffix_scores = jnp.einsum('cqd,cud->cqu', query_slab.astype(jnp.float32), suffix_key_set.astype(jnp.float32)) * factor
            live = lax.broadcasted_iota(jnp.int32, suffix_scores.shape, 2) < lengths[:, None, None]
            suffix_scores = jnp.where(live, suffix_scores, FAR_BELOW)
            highest = jnp.maximum(lax.optimization_barrier(jnp.max(prompt_scores, axis=1)), lax.optimization_barrier(jnp.max(suffix_scores, axis=2)).reshape(-1))
            prompt_weights = jnp.exp(prompt_scores - highest[:, None])
            suffix_weights = jnp.where(live, jnp.exp(suffix_scores - highest.reshape(CONT_DEV, QPK)[:, :, None]), 0.0)
            totals = lax.optimization_barrier(jnp.sum(prompt_weights, axis=1)) + lax.optimization_barrier(jnp.sum(suffix_weights, axis=2)).reshape(-1)
            numer = jnp.dot(prompt_weights.astype(jnp.bfloat16), value_block, preferred_element_type=jnp.float32)
            rounded_suffix = lax.optimization_barrier(suffix_weights.astype(jnp.bfloat16)).astype(jnp.float32)
            suffix_part = jnp.einsum('cqu,cud->cqd', rounded_suffix, suffix_value_set.astype(jnp.float32))
            numer = numer + suffix_part.reshape(CONT_DEV * QPK, HD)
            return (numer / totals[:, None]).astype(jnp.bfloat16).reshape(CONT_DEV, QPK, HD)
        return lax.map(block_attention, block_ids)
    stacked = lax.map(group_attention, group_ids)
    attended = jnp.transpose(stacked, (1, 2, 0, 3, 4)).reshape(CONT, HEADS, HD)
    projected = jnp.dot(attended.reshape(CONT, HEADS * HD), out_weight, preferred_element_type=jnp.float32).astype(jnp.bfloat16)
    return (attended, projected)
```

```python
import math

import jax
import jax.numpy as jnp
from jax import lax
from jax.sharding import PartitionSpec as P

FAR_BELOW = -1e30


def split_two(value):
    high = lax.reduce_precision(value, 8, 7)
    return high.astype(jnp.bfloat16), (value - high).astype(jnp.bfloat16)


def join_two(high, low):
    return high.astype(jnp.float32) + low.astype(jnp.float32)


def gathered(block, axes):
    count = lax.axis_size(axes)
    copies = jnp.broadcast_to(block[None], (count,) + block.shape)
    return lax.all_to_all(copies, axes, 0, 0, tiled=False)


def suffix_state(queries, suffix_keys, suffix_values, suffix_len, factor):
    cont_local, heads_local, head_dim = queries.shape
    key_set = suffix_keys[:, :, 0, :]
    value_set = suffix_values[:, :, 0, :]
    scores = (
        jnp.einsum("cqd,cud->cqu", queries, key_set, preferred_element_type=jnp.float32) * factor
    )
    live = lax.broadcasted_iota(jnp.int32, scores.shape, 2) < suffix_len[:, None, None]
    scores = jnp.where(live, scores, FAR_BELOW)
    highest = jnp.max(scores, axis=2)
    weights = jnp.where(live, jnp.exp(scores - highest[:, :, None]), 0.0)
    totals = jnp.sum(weights, axis=2)
    numer = jnp.einsum(
        "cqu,cud->cqd", weights.astype(jnp.bfloat16), value_set, preferred_element_type=jnp.float32
    )
    rows = cont_local * heads_local
    return (numer.reshape(rows, head_dim), highest.reshape(rows), totals.reshape(rows))


def body(queries, prompt_keys, prompt_values, suffix_keys, suffix_values, suffix_len, out_weight):
    cont_local, heads_local, head_dim = queries.shape
    factor = 1.0 / math.sqrt(head_dim)
    rows = cont_local * heads_local
    ctx = lax.axis_size("ctx")
    key_block = prompt_keys[:, 0, :]
    value_block = prompt_values[:, 0, :]
    home_numer, home_highest, home_totals = suffix_state(
        queries, suffix_keys, suffix_values, suffix_len, factor
    )

    with jax.named_scope("gather_queries"):
        visiting = gathered(queries.reshape(rows, head_dim), "ctx").reshape(ctx * rows, head_dim)
    with jax.named_scope("prompt_attention"):
        scores = (
            lax.dot_general(
                visiting, key_block, (((1,), (1,)), ((), ())), preferred_element_type=jnp.float32
            )
            * factor
        )
        highest = jnp.max(scores, axis=1)
        weights = jnp.exp(scores - highest[:, None])
        totals = jnp.sum(weights, axis=1)
        numer = jnp.dot(
            weights.astype(jnp.bfloat16), value_block, preferred_element_type=jnp.float32
        )
    with jax.named_scope("return_partials"):
        stats = jnp.stack(split_two(highest) + split_two(totals))
        stats = stats.reshape(4, ctx, rows).transpose(1, 0, 2).reshape(ctx, 4 * rows // head_dim, head_dim)
        sent = jnp.concatenate([numer.astype(jnp.bfloat16).reshape(ctx, rows, head_dim), stats], axis=1)
        back = lax.all_to_all(sent, "ctx", 0, 0, tiled=False)
    with jax.named_scope("combine"):
        numers = back[:, :rows].astype(jnp.float32)
        stats = back[:, rows:].reshape(ctx, 4, rows)
        highs = join_two(stats[:, 0], stats[:, 1])
        sums = join_two(stats[:, 2], stats[:, 3])
        joint = jnp.maximum(jnp.max(highs, axis=0), home_highest)
        scale = jnp.exp(highs - joint)
        home_scale = jnp.exp(home_highest - joint)
        total = jnp.sum(scale * sums, axis=0) + home_scale * home_totals
        numer = jnp.sum(scale[:, :, None] * numers, axis=0) + home_scale[:, None] * home_numer
        attended = (numer / total[:, None]).astype(jnp.bfloat16)
    attended_heads = attended.reshape(cont_local, heads_local, head_dim)
    with jax.named_scope("gather_attended"):
        flat_rows = attended.reshape(cont_local, heads_local * head_dim)
        everyone = gathered(flat_rows, ("ctx", "rep"))
        everyone = everyone.reshape(-1, heads_local * head_dim)
    with jax.named_scope("project"):
        terms = jnp.dot(everyone, out_weight, preferred_element_type=jnp.float32)
        terms = terms.astype(jnp.bfloat16)
    with jax.named_scope("sum_heads"):
        kvh = lax.axis_size("kvh")
        terms = terms.reshape(kvh, terms.shape[0] // kvh, terms.shape[1])
        parts = lax.all_to_all(terms, "kvh", 0, 0, tiled=False)
        projected = jnp.sum(parts.astype(jnp.float32), axis=0).astype(jnp.bfloat16)
    return (attended_heads, projected)


def solution(mesh):
    in_specs = (
        P(("ctx", "rep"), "kvh", None),
        P("ctx", "kvh", None),
        P("ctx", "kvh", None),
        P(("ctx", "rep"), None, "kvh", None),
        P(("ctx", "rep"), None, "kvh", None),
        P(("ctx", "rep")),
        P("kvh", ("ctx", "rep")),
    )
    out_specs = (P(("ctx", "rep"), "kvh", None), P("kvh", ("ctx", "rep")))
    return jax.shard_map(body, mesh=mesh, in_specs=in_specs, out_specs=out_specs, check_vma=False)
```

```python
import functools
import math

import jax
import jax.numpy as jnp
from jax import lax
from jax.experimental import pallas as pl
from jax.experimental.pallas import tpu as pltpu
from jax.sharding import Mesh
from jax.sharding import PartitionSpec as P

FAR_BELOW = -1e30
CTX = ("y", "zl")
KVH = ("x", "core")
REP = ("zh",)
VMEM = pl.BlockSpec(memory_space=pltpu.VMEM)
SMEM = pl.BlockSpec(memory_space=pltpu.SMEM)
LAST_WITH_LAST = (((1,), (1,)), ((), ()))
FIRST_WITH_FIRST = (((0,), (0,)), ((), ()))
STAT_ROWS = 16


def base_two(head_dim):
    return math.log2(math.e) / math.sqrt(head_dim)


def gathered(copies, axes):
    return lax.all_to_all(copies, axes, 0, 0, tiled=False)


def suffix_kernel(len_ref, query_ref, key_ref, value_ref, numer_ref, stat_ref, *, conts):
    rows, head_dim = query_ref.shape
    slots = key_ref.shape[0] // conts
    twice = jnp.concatenate([query_ref[...]] * 2, axis=0)
    scores = lax.dot_general(
        key_ref[...], twice, LAST_WITH_LAST, preferred_element_type=jnp.float32
    )
    scores = scores.reshape(conts, slots, 2 * rows)
    lane = lax.broadcasted_iota(jnp.int32, (1, 2 * rows), 1) % rows
    place = lax.broadcasted_iota(jnp.int32, (slots, 2 * rows), 0)
    per_cont = rows // conts
    masked = []
    for c in range(conts):
        limit = jnp.where(lane // per_cont == c, len_ref[c], 0)
        masked.append(jnp.where(place < limit, scores[c], FAR_BELOW))
    scores = jnp.concatenate(masked, axis=0)
    highest = jnp.max(scores, axis=0, keepdims=True)
    weights = jnp.where(
        scores > 0.5 * FAR_BELOW, jnp.exp2((scores - highest) * base_two(head_dim)), 0.0
    )
    totals = jnp.sum(weights, axis=0, keepdims=True)
    numer = lax.dot_general(
        value_ref[...],
        weights.astype(jnp.bfloat16),
        FIRST_WITH_FIRST,
        preferred_element_type=jnp.float32,
    )
    numer_ref[...] = numer.T[:rows]
    stat_ref[...] = jnp.concatenate(
        [highest, totals, jnp.zeros((6, 2 * rows), jnp.float32)], axis=0
    )


def prompt_kernel(query_ref, key_ref, value_ref, out_ref):
    blocks, block_rows, head_dim = query_ref.shape
    rows = blocks * block_rows
    queries = query_ref[...].reshape(rows, head_dim)
    scores = lax.dot_general(
        key_ref[...], queries, LAST_WITH_LAST, preferred_element_type=jnp.float32
    )
    shift = jnp.max(scores, axis=0, keepdims=True).astype(jnp.bfloat16)
    weights = jnp.exp2((scores - shift.astype(jnp.float32)) * base_two(head_dim))
    totals = jnp.sum(weights, axis=0, keepdims=True)
    numer = lax.dot_general(
        value_ref[...],
        weights.astype(jnp.bfloat16),
        FIRST_WITH_FIRST,
        preferred_element_type=jnp.float32,
    )
    out_ref[:, :block_rows, :] = (
        numer.T.astype(jnp.bfloat16).reshape(blocks, block_rows, head_dim)
    )
    high = totals.astype(jnp.bfloat16)
    low = totals - high.astype(jnp.float32)
    stats = jnp.concatenate(
        [
            shift.astype(jnp.float32),
            high.astype(jnp.float32),
            low,
            jnp.zeros((STAT_ROWS - 3, rows), jnp.float32),
        ],
        axis=0,
    ).astype(jnp.bfloat16)
    for block in range(blocks):
        tile = block * block_rows // head_dim
        out_ref[block, block_rows:, :] = stats[:, tile * head_dim : (tile + 1) * head_dim]


def combine_kernel(half_ref, back_ref, numer_ref, stat_ref, out_ref, spread_ref):
    blocks, _, head_dim = back_ref.shape
    rows = out_ref.shape[0]
    stats = back_ref[:, rows:, :].astype(jnp.float32)
    highs = stats[:, 0, :]
    sums = stats[:, 1, :] + stats[:, 2, :]
    home_high = stat_ref[0:1, :]
    home_sum = stat_ref[1:2, :]
    joint = jnp.maximum(jnp.max(highs, axis=0, keepdims=True), home_high)
    scale = jnp.exp2((highs - joint) * base_two(head_dim))
    home_scale = jnp.exp2((home_high - joint) * base_two(head_dim))
    total = jnp.sum(scale * sums, axis=0, keepdims=True) + home_scale * home_sum
    factors = jnp.concatenate(
        [
            scale / total,
            home_scale / total,
            jnp.zeros((head_dim - blocks - 1, head_dim), jnp.float32),
        ],
        axis=0,
    )
    spread_ref[...] = factors.T
    factors = spread_ref[pl.ds(pl.multiple_of(half_ref[0] * rows, rows), rows), :]
    numer = numer_ref[...] * factors[:, blocks : blocks + 1]
    for block in range(blocks):
        numer += back_ref[block, :rows, :].astype(jnp.float32) * factors[:, block : block + 1]
    out_ref[...] = numer.astype(jnp.bfloat16)


def body(queries, prompt_keys, prompt_values, suffix_keys, suffix_values, suffix_len, out_weight):
    conts, heads, head_dim = queries.shape
    rows = conts * heads
    ctx = lax.axis_size(CTX)
    rep = lax.axis_size(REP)
    kvh = lax.axis_size(KVH)
    half = lax.axis_index("zl")
    tokens = prompt_keys.shape[0]
    slots = suffix_keys.shape[1]
    depth, width = out_weight.shape
    params = pltpu.CompilerParams(vmem_limit_bytes=48 * 2**20)
    query_rows = queries.reshape(rows, head_dim)

    with jax.named_scope("gather_queries"):
        visiting = gathered(
            jnp.broadcast_to(query_rows[None], (ctx, rows, head_dim)), CTX
        )
    with jax.named_scope("swap_weight"):
        halves = out_weight.reshape(2, depth // 2, width)
        kept = lax.dynamic_index_in_dim(halves, half, 0, keepdims=False)
        given = lax.dynamic_index_in_dim(halves, 1 - half, 0, keepdims=False)
        taken = lax.ppermute(given, "zl", [(0, 1), (1, 0)])
    with jax.named_scope("suffix_attention"):
        home_numer, home_stat = pl.pallas_call(
            functools.partial(suffix_kernel, conts=conts),
            in_specs=[SMEM, VMEM, VMEM, VMEM],
            out_specs=[VMEM, VMEM],
            out_shape=[
                jax.ShapeDtypeStruct((rows, head_dim), jnp.float32),
                jax.ShapeDtypeStruct((8, head_dim), jnp.float32),
            ],
            compiler_params=params,
            cost_estimate=pl.CostEstimate(
                flops=4 * conts * slots * head_dim * head_dim,
                bytes_accessed=4 * conts * slots * head_dim,
                transcendentals=conts * slots * head_dim,
            ),
        )(
            suffix_len,
            query_rows,
            suffix_keys.reshape(conts * slots, head_dim),
            suffix_values.reshape(conts * slots, head_dim),
        )
    with jax.named_scope("prompt_attention"):
        sent = pl.pallas_call(
            prompt_kernel,
            in_specs=[VMEM] * 3,
            out_specs=VMEM,
            out_shape=jax.ShapeDtypeStruct((ctx, rows + STAT_ROWS, head_dim), jnp.bfloat16),
            compiler_params=params,
            cost_estimate=pl.CostEstimate(
                flops=4 * ctx * rows * tokens * head_dim,
                bytes_accessed=4 * tokens * head_dim,
                transcendentals=ctx * rows * tokens,
            ),
        )(
            visiting,
            prompt_keys.reshape(tokens, head_dim),
            prompt_values.reshape(tokens, head_dim),
        )
    with jax.named_scope("return_partials"):
        back = lax.all_to_all(sent, CTX, 0, 0, tiled=False)
    with jax.named_scope("combine"):
        attended = pl.pallas_call(
            combine_kernel,
            in_specs=[SMEM, VMEM, VMEM, VMEM],
            out_specs=VMEM,
            out_shape=jax.ShapeDtypeStruct((rows, head_dim), jnp.bfloat16),
            scratch_shapes=[pltpu.VMEM((head_dim, head_dim), jnp.float32)],
            compiler_params=params,
        )(half.reshape(1), back, home_numer, home_stat)
    with jax.named_scope("gather_attended"):
        flat = attended.reshape(conts, 2, depth // 2).transpose(1, 0, 2)
        copies = jnp.broadcast_to(
            flat[None, :, None], (ctx // 2, 2, rep, conts, depth // 2)
        ).reshape(ctx * rep, conts, depth // 2)
        everyone = gathered(copies, CTX + REP).reshape(ctx * rep * conts, depth // 2)
    with jax.named_scope("project"):
        own = jnp.dot(everyone, kept, preferred_element_type=jnp.float32)
        other = jnp.dot(everyone, taken, preferred_element_type=jnp.float32)
        own, other = own.astype(jnp.bfloat16), other.astype(jnp.bfloat16)
    with jax.named_scope("sum_heads"):
        low = jnp.where(half == 0, own, other).reshape(kvh, -1, width)
        high = jnp.where(half == 0, other, own).reshape(kvh, -1, width)
        terms = jnp.stack([low, high], axis=1).reshape(2 * kvh, -1, width)
        parts = lax.all_to_all(terms, KVH + ("zl",), 0, 0, tiled=False)
        projected = jnp.sum(parts.astype(jnp.float32), axis=0).astype(jnp.bfloat16)
    return (attended.reshape(conts, heads, head_dim), projected)


def solution(mesh):
    ctx, kvh, rep = (mesh.shape[name] for name in ("ctx", "kvh", "rep"))
    fine = Mesh(
        mesh.devices.reshape(ctx // 2, 2, kvh // 2, 2, rep), ("y", "zl", "x", "core", "zh")
    )
    groups = CTX + REP
    in_specs = (
        P(groups, KVH, None),
        P(CTX, KVH, None),
        P(CTX, KVH, None),
        P(groups, None, KVH, None),
        P(groups, None, KVH, None),
        P(groups),
        P(KVH, groups),
    )
    out_specs = (P(groups, KVH, None), P(KVH, groups))
    return jax.shard_map(body, mesh=fine, in_specs=in_specs, out_specs=out_specs, check_vma=False)
```

```python
import functools
import math

import jax
import jax.numpy as jnp
from jax import lax
from jax.experimental import pallas as pl
from jax.experimental.pallas import tpu as pltpu
from jax.sharding import Mesh
from jax.sharding import PartitionSpec as P

FAR_BELOW = -1e30
CTX = ("y", "zl")
KVH = ("x", "core")
REP = ("zh",)
VMEM = pl.BlockSpec(memory_space=pltpu.VMEM)
SMEM = pl.BlockSpec(memory_space=pltpu.SMEM)
LAST_WITH_LAST = (((1,), (1,)), ((), ()))
FIRST_WITH_FIRST = (((0,), (0,)), ((), ()))
STAT_ROWS = 16


def base_two(head_dim):
    return math.log2(math.e) / math.sqrt(head_dim)


def gathered(copies, axes):
    return lax.all_to_all(copies, axes, 0, 0, tiled=False)


def suffix_kernel(len_ref, query_ref, key_ref, value_ref, numer_ref, stat_ref, *, conts):
    rows, head_dim = query_ref.shape
    slots = key_ref.shape[0] // conts
    twice = jnp.concatenate([query_ref[...]] * 2, axis=0)
    scores = lax.dot_general(
        key_ref[...], twice, LAST_WITH_LAST, preferred_element_type=jnp.float32
    )
    scores = scores.reshape(conts, slots, 2 * rows)
    lane = lax.broadcasted_iota(jnp.int32, (1, 2 * rows), 1) % rows
    place = lax.broadcasted_iota(jnp.int32, (slots, 2 * rows), 0)
    per_cont = rows // conts
    masked = []
    for c in range(conts):
        limit = jnp.where(lane // per_cont == c, len_ref[c], 0)
        masked.append(jnp.where(place < limit, scores[c], FAR_BELOW))
    scores = jnp.concatenate(masked, axis=0)
    highest = jnp.max(scores, axis=0, keepdims=True)
    weights = jnp.where(
        scores > 0.5 * FAR_BELOW, jnp.exp2((scores - highest) * base_two(head_dim)), 0.0
    )
    totals = jnp.sum(weights, axis=0, keepdims=True)
    numer = lax.dot_general(
        value_ref[...],
        weights.astype(jnp.bfloat16),
        FIRST_WITH_FIRST,
        preferred_element_type=jnp.float32,
    )
    numer_ref[...] = numer.T[:rows]
    stat_ref[...] = jnp.concatenate(
        [highest, totals, jnp.zeros((6, 2 * rows), jnp.float32)], axis=0
    )


def prompt_kernel(query_ref, key_ref, value_hbm, out_ref, value_ref, value_sem):
    blocks, block_rows, head_dim = query_ref.shape
    rows = blocks * block_rows
    copy = pltpu.make_async_copy(value_hbm, value_ref, value_sem)
    copy.start()
    queries = query_ref[...].reshape(rows, head_dim)
    scores = lax.dot_general(
        key_ref[...], queries, LAST_WITH_LAST, preferred_element_type=jnp.float32
    )
    shift = jnp.max(scores, axis=0, keepdims=True).astype(jnp.bfloat16)
    weights = jnp.exp2((scores - shift.astype(jnp.float32)) * base_two(head_dim))
    totals = jnp.sum(weights, axis=0, keepdims=True)
    copy.wait()
    numer = lax.dot_general(
        value_ref[...],
        weights.astype(jnp.bfloat16),
        FIRST_WITH_FIRST,
        preferred_element_type=jnp.float32,
    )
    out_ref[:, :block_rows, :] = (
        numer.T.astype(jnp.bfloat16).reshape(blocks, block_rows, head_dim)
    )
    high = totals.astype(jnp.bfloat16)
    low = totals - high.astype(jnp.float32)
    stats = jnp.concatenate(
        [
            shift.astype(jnp.float32),
            high.astype(jnp.float32),
            low,
            jnp.zeros((STAT_ROWS - 3, rows), jnp.float32),
        ],
        axis=0,
    ).astype(jnp.bfloat16)
    for block in range(blocks):
        tile = block * block_rows // head_dim
        out_ref[block, block_rows:, :] = stats[:, tile * head_dim : (tile + 1) * head_dim]


def combine_kernel(half_ref, back_ref, numer_ref, stat_ref, out_ref, copies_ref, spread_ref, *, rep):
    blocks, _, head_dim = back_ref.shape
    rows = out_ref.shape[0]
    stats = back_ref[:, rows:, :].astype(jnp.float32)
    highs = stats[:, 0, :]
    sums = stats[:, 1, :] + stats[:, 2, :]
    home_high = stat_ref[0:1, :]
    home_sum = stat_ref[1:2, :]
    joint = jnp.maximum(jnp.max(highs, axis=0, keepdims=True), home_high)
    scale = jnp.exp2((highs - joint) * base_two(head_dim))
    home_scale = jnp.exp2((home_high - joint) * base_two(head_dim))
    total = jnp.sum(scale * sums, axis=0, keepdims=True) + home_scale * home_sum
    factors = jnp.concatenate(
        [
            scale / total,
            home_scale / total,
            jnp.zeros((head_dim - blocks - 1, head_dim), jnp.float32),
        ],
        axis=0,
    )
    spread_ref[...] = factors.T
    factors = spread_ref[pl.ds(pl.multiple_of(half_ref[0] * rows, rows), rows), :]
    numer = numer_ref[...] * factors[:, blocks : blocks + 1]
    for block in range(blocks):
        numer += back_ref[block, :rows, :].astype(jnp.float32) * factors[:, block : block + 1]
    out_ref[...] = numer.astype(jnp.bfloat16)
    slabs = numer.reshape(-1, 2, 8, head_dim)
    parts = [
        slabs[:, part].reshape(rows // 2, head_dim).astype(jnp.bfloat16) for part in range(2)
    ]
    for place in range(copies_ref.shape[0]):
        copies_ref[place] = parts[place // rep % 2]


def project_kernel(half_ref, block_ref, weight_ref, taken_ref, out_ref, wide_ref):
    places, block_rows, head_dim = block_ref.shape
    wide_ref[...] = block_ref[...].reshape(places * block_rows, head_dim).astype(jnp.float32)
    heads = weight_ref.shape[0] // (2 * head_dim)
    conts = places * block_rows // heads
    left = jnp.concatenate(
        [
            wide_ref[pl.ds(head, conts, stride=heads), :].astype(jnp.bfloat16)
            for head in range(heads)
        ],
        axis=1,
    )
    half = half_ref[0]
    depth = heads * head_dim
    kept = weight_ref[pl.ds(pl.multiple_of(half * depth, depth), depth), :]
    own = jnp.dot(left, kept, preferred_element_type=jnp.float32).astype(jnp.bfloat16)
    other = jnp.dot(left, taken_ref[...], preferred_element_type=jnp.float32).astype(jnp.bfloat16)
    out_rows = out_ref.shape[1]
    for group in range(out_ref.shape[0] // 2):
        rows = slice(group * out_rows, (group + 1) * out_rows)
        out_ref[2 * group + half] = own[rows]
        out_ref[2 * group + 1 - half] = other[rows]


def body(queries, prompt_keys, prompt_values, suffix_keys, suffix_values, suffix_len, out_weight):
    conts, heads, head_dim = queries.shape
    rows = conts * heads
    ctx = lax.axis_size(CTX)
    rep = lax.axis_size(REP)
    kvh = lax.axis_size(KVH)
    half = lax.axis_index("zl")
    tokens = prompt_keys.shape[0]
    slots = suffix_keys.shape[1]
    depth, width = out_weight.shape
    large = pltpu.CompilerParams(vmem_limit_bytes=40 * 2**20)
    small = pltpu.CompilerParams(vmem_limit_bytes=12 * 2**20)
    query_rows = queries.reshape(rows, head_dim)

    with jax.named_scope("gather_queries"):
        visiting = gathered(
            jnp.broadcast_to(query_rows[None], (ctx, rows, head_dim)), CTX
        )
    with jax.named_scope("swap_weight"):
        halves = out_weight.reshape(2, depth // 2, width)
        given = lax.dynamic_index_in_dim(halves, 1 - half, 0, keepdims=False)
        taken = lax.ppermute(given, "zl", [(0, 1), (1, 0)])
    with jax.named_scope("suffix_attention"):
        home_numer, home_stat = pl.pallas_call(
            functools.partial(suffix_kernel, conts=conts),
            in_specs=[SMEM, VMEM, VMEM, VMEM],
            out_specs=[VMEM, VMEM],
            out_shape=[
                jax.ShapeDtypeStruct((rows, head_dim), jnp.float32),
                jax.ShapeDtypeStruct((8, head_dim), jnp.float32),
            ],
            compiler_params=small,
            cost_estimate=pl.CostEstimate(
                flops=4 * conts * slots * head_dim * head_dim,
                bytes_accessed=4 * conts * slots * head_dim,
                transcendentals=conts * slots * head_dim,
            ),
        )(
            suffix_len,
            query_rows,
            suffix_keys.reshape(conts * slots, head_dim),
            suffix_values.reshape(conts * slots, head_dim),
        )
    visiting, home_numer, home_stat, taken = lax.optimization_barrier(
        (visiting, home_numer, home_stat, taken)
    )
    with jax.named_scope("prompt_attention"):
        sent = pl.pallas_call(
            prompt_kernel,
            in_specs=[VMEM, VMEM, pl.BlockSpec(memory_space=pltpu.HBM)],
            out_specs=VMEM,
            scratch_shapes=[
                pltpu.VMEM((tokens, head_dim), jnp.bfloat16),
                pltpu.SemaphoreType.DMA,
            ],
            out_shape=jax.ShapeDtypeStruct((ctx, rows + STAT_ROWS, head_dim), jnp.bfloat16),
            compiler_params=large,
            cost_estimate=pl.CostEstimate(
                flops=4 * ctx * rows * tokens * head_dim,
                bytes_accessed=4 * tokens * head_dim,
                transcendentals=ctx * rows * tokens,
            ),
        )(
            visiting,
            prompt_keys.reshape(tokens, head_dim),
            pltpu.with_memory_space_constraint(
                prompt_values.reshape(tokens, head_dim), pltpu.HBM
            ),
        )
    with jax.named_scope("return_partials"):
        back = lax.all_to_all(sent, CTX, 0, 0, tiled=False)
    with jax.named_scope("combine"):
        attended, copies = pl.pallas_call(
            functools.partial(combine_kernel, rep=rep),
            in_specs=[SMEM, VMEM, VMEM, VMEM],
            out_specs=[VMEM, VMEM],
            out_shape=[
                jax.ShapeDtypeStruct((rows, head_dim), jnp.bfloat16),
                jax.ShapeDtypeStruct((ctx * rep, rows // 2, head_dim), jnp.bfloat16),
            ],
            scratch_shapes=[pltpu.VMEM((head_dim, head_dim), jnp.float32)],
            compiler_params=small,
        )(half.reshape(1), back, home_numer, home_stat)
    with jax.named_scope("gather_attended"):
        everyone = lax.all_to_all(copies, CTX + REP, 0, 0, tiled=False)
    with jax.named_scope("project"):
        terms = pl.pallas_call(
            project_kernel,
            in_specs=[SMEM, VMEM, VMEM, VMEM],
            out_specs=VMEM,
            out_shape=jax.ShapeDtypeStruct(
                (2 * kvh, ctx * rep * conts // kvh, width), jnp.bfloat16
            ),
            scratch_shapes=[pltpu.VMEM((ctx * rep * rows // 2, head_dim), jnp.float32)],
            compiler_params=small,
        )(half.reshape(1), everyone, out_weight, taken)
    with jax.named_scope("sum_heads"):
        parts = lax.all_to_all(terms, KVH + ("zl",), 0, 0, tiled=False)
        projected = jnp.sum(parts.astype(jnp.float32), axis=0).astype(jnp.bfloat16)
    return (attended.reshape(conts, heads, head_dim), projected)


def solution(mesh):
    ctx, kvh, rep = (mesh.shape[name] for name in ("ctx", "kvh", "rep"))
    fine = Mesh(
        mesh.devices.reshape(ctx // 2, 2, kvh // 2, 2, rep), ("y", "zl", "x", "core", "zh")
    )
    groups = CTX + REP
    in_specs = (
        P(groups, KVH, None),
        P(CTX, KVH, None),
        P(CTX, KVH, None),
        P(groups, None, KVH, None),
        P(groups, None, KVH, None),
        P(groups),
        P(KVH, groups),
    )
    out_specs = (P(groups, KVH, None), P(KVH, groups))
    return jax.shard_map(body, mesh=fine, in_specs=in_specs, out_specs=out_specs, check_vma=False)
```

```python
import functools
import math

import jax
import jax.numpy as jnp
from jax import lax
from jax.experimental import pallas as pl
from jax.experimental.pallas import tpu as pltpu
from jax.sharding import Mesh
from jax.sharding import PartitionSpec as P

FAR_BELOW = -1e30
CTX = ("y", "zl")
KVH = ("x", "core")
REP = ("zh",)
VMEM = pl.BlockSpec(memory_space=pltpu.VMEM)
SMEM = pl.BlockSpec(memory_space=pltpu.SMEM)
LAST_WITH_LAST = (((1,), (1,)), ((), ()))
FIRST_WITH_FIRST = (((0,), (0,)), ((), ()))
STAT_ROWS = 8


def base_two(head_dim):
    return math.log2(math.e) / math.sqrt(head_dim)


def gathered(copies, axes):
    return lax.all_to_all(copies, axes, 0, 0, tiled=False)


def suffix_kernel(len_ref, query_ref, key_ref, value_ref, numer_ref, stat_ref, *, conts):
    rows, head_dim = query_ref.shape
    slots = key_ref.shape[0] // conts
    twice = jnp.concatenate([query_ref[...]] * 2, axis=0)
    scores = lax.dot_general(
        key_ref[...], twice, LAST_WITH_LAST, preferred_element_type=jnp.float32
    )
    scores = scores.reshape(conts, slots, 2 * rows)
    lane = lax.broadcasted_iota(jnp.int32, (1, 2 * rows), 1) % rows
    place = lax.broadcasted_iota(jnp.int32, (slots, 2 * rows), 0)
    per_cont = rows // conts
    masked = []
    for c in range(conts):
        limit = jnp.where(lane // per_cont == c, len_ref[c], 0)
        masked.append(jnp.where(place < limit, scores[c], FAR_BELOW))
    scores = jnp.concatenate(masked, axis=0)
    highest = jnp.max(scores, axis=0, keepdims=True)
    weights = jnp.where(
        scores > 0.5 * FAR_BELOW, jnp.exp2((scores - highest) * base_two(head_dim)), 0.0
    )
    totals = jnp.sum(weights, axis=0, keepdims=True)
    numer = lax.dot_general(
        value_ref[...],
        weights.astype(jnp.bfloat16),
        FIRST_WITH_FIRST,
        preferred_element_type=jnp.float32,
    )
    numer_ref[...] = numer.T[:rows]
    stat_ref[...] = jnp.concatenate(
        [highest, totals, jnp.zeros((6, 2 * rows), jnp.float32)], axis=0
    )


def prompt_kernel(query_ref, key_ref, value_hbm, out_ref, value_ref, value_sem):
    blocks, block_rows, head_dim = query_ref.shape
    rows = blocks * block_rows
    copy = pltpu.make_async_copy(value_hbm, value_ref, value_sem)
    copy.start()
    queries = query_ref[...].reshape(rows, head_dim)
    scores = lax.dot_general(
        key_ref[...], queries, LAST_WITH_LAST, preferred_element_type=jnp.float32
    )
    shift = jnp.max(scores, axis=0, keepdims=True).astype(jnp.bfloat16)
    weights = jnp.exp2((scores - shift.astype(jnp.float32)) * base_two(head_dim))
    totals = jnp.sum(weights, axis=0, keepdims=True)
    copy.wait()
    numer = lax.dot_general(
        value_ref[...],
        weights.astype(jnp.bfloat16),
        FIRST_WITH_FIRST,
        preferred_element_type=jnp.float32,
    )
    out_ref[:, :block_rows, :] = (
        numer.T.astype(jnp.bfloat16).reshape(blocks, block_rows, head_dim)
    )
    high = totals.astype(jnp.bfloat16)
    low = totals - high.astype(jnp.float32)
    stats = jnp.concatenate(
        [
            shift.astype(jnp.float32),
            high.astype(jnp.float32),
            low,
            jnp.zeros((STAT_ROWS - 3, rows), jnp.float32),
        ],
        axis=0,
    ).astype(jnp.bfloat16)
    for block in range(blocks):
        tile = block * block_rows // head_dim
        out_ref[block, block_rows:, :] = stats[:, tile * head_dim : (tile + 1) * head_dim]


def combine_kernel(half_ref, back_ref, numer_ref, stat_ref, out_ref, copies_ref, spread_ref, *, rep):
    blocks, _, head_dim = back_ref.shape
    rows = out_ref.shape[0]
    stats = back_ref[:, rows:, :].astype(jnp.float32)
    highs = stats[:, 0, :]
    sums = stats[:, 1, :] + stats[:, 2, :]
    home_high = stat_ref[0:1, :]
    home_sum = stat_ref[1:2, :]
    joint = jnp.maximum(jnp.max(highs, axis=0, keepdims=True), home_high)
    scale = jnp.exp2((highs - joint) * base_two(head_dim))
    home_scale = jnp.exp2((home_high - joint) * base_two(head_dim))
    total = jnp.sum(scale * sums, axis=0, keepdims=True) + home_scale * home_sum
    factors = jnp.concatenate(
        [
            scale / total,
            home_scale / total,
            jnp.zeros((head_dim - blocks - 1, head_dim), jnp.float32),
        ],
        axis=0,
    )
    spread_ref[...] = factors.T
    factors = spread_ref[pl.ds(pl.multiple_of(half_ref[0] * rows, rows), rows), :]
    numer = numer_ref[...] * factors[:, blocks : blocks + 1]
    for block in range(blocks):
        numer += back_ref[block, :rows, :].astype(jnp.float32) * factors[:, block : block + 1]
    out_ref[...] = numer.astype(jnp.bfloat16)
    slabs = numer.reshape(-1, 2, 8, head_dim)
    parts = [
        slabs[:, part].reshape(rows // 2, head_dim).astype(jnp.bfloat16) for part in range(2)
    ]
    for place in range(copies_ref.shape[0]):
        copies_ref[place] = parts[place // rep % 2]


def project_kernel(half_ref, block_ref, weight_ref, upper_ref, lower_ref, out_ref, wide_ref):
    places, block_rows, head_dim = block_ref.shape
    wide_ref[...] = block_ref[...].reshape(places * block_rows, head_dim).astype(jnp.float32)
    heads = weight_ref.shape[0] // (2 * head_dim)
    conts = places * block_rows // heads
    left = jnp.concatenate(
        [
            wide_ref[pl.ds(head, conts, stride=heads), :].astype(jnp.bfloat16)
            for head in range(heads)
        ],
        axis=1,
    )
    half = half_ref[0]
    depth = heads * head_dim
    kept = weight_ref[pl.ds(pl.multiple_of(half * depth, depth), depth), :]
    own = jnp.dot(left, kept, preferred_element_type=jnp.float32).astype(jnp.bfloat16)
    cut = upper_ref.shape[0]
    other = jnp.dot(left[:, :cut], upper_ref[...], preferred_element_type=jnp.float32)
    other += jnp.dot(left[:, cut:], lower_ref[...], preferred_element_type=jnp.float32)
    other = other.astype(jnp.bfloat16)
    out_rows = out_ref.shape[1]
    for group in range(out_ref.shape[0] // 2):
        rows = slice(group * out_rows, (group + 1) * out_rows)
        out_ref[2 * group + half] = own[rows]
        out_ref[2 * group + 1 - half] = other[rows]


def body(queries, prompt_keys, prompt_values, suffix_keys, suffix_values, suffix_len, out_weight):
    conts, heads, head_dim = queries.shape
    rows = conts * heads
    ctx = lax.axis_size(CTX)
    rep = lax.axis_size(REP)
    kvh = lax.axis_size(KVH)
    half = lax.axis_index("zl")
    tokens = prompt_keys.shape[0]
    slots = suffix_keys.shape[1]
    depth, width = out_weight.shape
    large = pltpu.CompilerParams(vmem_limit_bytes=40 * 2**20)
    small = pltpu.CompilerParams(vmem_limit_bytes=12 * 2**20)
    query_rows = queries.reshape(rows, head_dim)

    with jax.named_scope("gather_queries"):
        visiting = gathered(
            jnp.broadcast_to(query_rows[None], (ctx, rows, head_dim)), CTX
        )
    with jax.named_scope("swap_weight"):
        halves = out_weight.reshape(2, depth // 2, width)
        given = lax.dynamic_index_in_dim(halves, 1 - half, 0, keepdims=False)
        cut = depth // 8 * 3
        taken = [
            lax.ppermute(part, "zl", [(0, 1), (1, 0)]) for part in (given[:cut], given[cut:])
        ]
    with jax.named_scope("suffix_attention"):
        home_numer, home_stat = pl.pallas_call(
            functools.partial(suffix_kernel, conts=conts),
            in_specs=[SMEM, VMEM, VMEM, VMEM],
            out_specs=[VMEM, VMEM],
            out_shape=[
                jax.ShapeDtypeStruct((rows, head_dim), jnp.float32),
                jax.ShapeDtypeStruct((8, head_dim), jnp.float32),
            ],
            compiler_params=small,
            cost_estimate=pl.CostEstimate(
                flops=4 * conts * slots * head_dim * head_dim,
                bytes_accessed=4 * conts * slots * head_dim,
                transcendentals=conts * slots * head_dim,
            ),
        )(
            suffix_len,
            query_rows,
            suffix_keys.reshape(conts * slots, head_dim),
            suffix_values.reshape(conts * slots, head_dim),
        )
    visiting, home_numer, home_stat = lax.optimization_barrier(
        (visiting, home_numer, home_stat)
    )
    with jax.named_scope("prompt_attention"):
        sent = pl.pallas_call(
            prompt_kernel,
            in_specs=[VMEM, VMEM, pl.BlockSpec(memory_space=pltpu.HBM)],
            out_specs=VMEM,
            scratch_shapes=[
                pltpu.VMEM((tokens, head_dim), jnp.bfloat16),
                pltpu.SemaphoreType.DMA,
            ],
            out_shape=jax.ShapeDtypeStruct((ctx, rows + STAT_ROWS, head_dim), jnp.bfloat16),
            compiler_params=large,
            cost_estimate=pl.CostEstimate(
                flops=4 * ctx * rows * tokens * head_dim,
                bytes_accessed=4 * tokens * head_dim,
                transcendentals=ctx * rows * tokens,
            ),
        )(
            visiting,
            prompt_keys.reshape(tokens, head_dim),
            pltpu.with_memory_space_constraint(
                prompt_values.reshape(tokens, head_dim), pltpu.HBM
            ),
        )
    sent, taken[0] = lax.optimization_barrier((sent, taken[0]))
    with jax.named_scope("return_partials"):
        back = lax.all_to_all(sent, CTX, 0, 0, tiled=False)
    with jax.named_scope("combine"):
        attended, copies = pl.pallas_call(
            functools.partial(combine_kernel, rep=rep),
            in_specs=[SMEM, VMEM, VMEM, VMEM],
            out_specs=[VMEM, VMEM],
            out_shape=[
                jax.ShapeDtypeStruct((rows, head_dim), jnp.bfloat16),
                jax.ShapeDtypeStruct((ctx * rep, rows // 2, head_dim), jnp.bfloat16),
            ],
            scratch_shapes=[pltpu.VMEM((head_dim, head_dim), jnp.float32)],
            compiler_params=small,
        )(half.reshape(1), back, home_numer, home_stat)
    copies, taken[1] = lax.optimization_barrier((copies, taken[1]))
    with jax.named_scope("gather_attended"):
        everyone = lax.all_to_all(copies, CTX + REP, 0, 0, tiled=False)
    with jax.named_scope("project"):
        terms = pl.pallas_call(
            project_kernel,
            in_specs=[SMEM, VMEM, VMEM, VMEM, VMEM],
            out_specs=VMEM,
            out_shape=jax.ShapeDtypeStruct(
                (2 * kvh, ctx * rep * conts // kvh, width), jnp.bfloat16
            ),
            scratch_shapes=[pltpu.VMEM((ctx * rep * rows // 2, head_dim), jnp.float32)],
            compiler_params=small,
        )(half.reshape(1), everyone, out_weight, taken[0], taken[1])
    with jax.named_scope("sum_heads"):
        parts = lax.all_to_all(terms, KVH + ("zl",), 0, 0, tiled=False)
        projected = jnp.sum(parts.astype(jnp.float32), axis=0).astype(jnp.bfloat16)
    return (attended.reshape(conts, heads, head_dim), projected)


def solution(mesh):
    ctx, kvh, rep = (mesh.shape[name] for name in ("ctx", "kvh", "rep"))
    fine = Mesh(
        mesh.devices.reshape(ctx // 2, 2, kvh // 2, 2, rep), ("y", "zl", "x", "core", "zh")
    )
    groups = CTX + REP
    in_specs = (
        P(groups, KVH, None),
        P(CTX, KVH, None),
        P(CTX, KVH, None),
        P(groups, None, KVH, None),
        P(groups, None, KVH, None),
        P(groups),
        P(KVH, groups),
    )
    out_specs = (P(groups, KVH, None), P(KVH, groups))
    return jax.shard_map(body, mesh=fine, in_specs=in_specs, out_specs=out_specs, check_vma=False)
```

```python
import functools
import math

import jax
import jax.numpy as jnp
from jax import lax
from jax.experimental import pallas as pl
from jax.experimental.pallas import tpu as pltpu
from jax.sharding import Mesh
from jax.sharding import PartitionSpec as P

FAR_BELOW = -1e30
CTX = ("y", "zl")
KVH = ("x", "core")
REP = ("zh",)
VMEM = pl.BlockSpec(memory_space=pltpu.VMEM)
HBM = pl.BlockSpec(memory_space=pltpu.HBM)
SMEM = pl.BlockSpec(memory_space=pltpu.SMEM)
LAST_WITH_LAST = (((1,), (1,)), ((), ()))
FIRST_WITH_FIRST = (((0,), (0,)), ((), ()))
STAT_ROWS = 8


def base_two(head_dim):
    return math.log2(math.e) / math.sqrt(head_dim)


def suffix_kernel(len_ref, query_ref, key_ref, value_ref, numer_ref, stat_ref, *, conts):
    rows, head_dim = query_ref.shape
    slots = key_ref.shape[0] // conts
    twice = jnp.concatenate([query_ref[...]] * 2, axis=0)
    scores = lax.dot_general(
        key_ref[...], twice, LAST_WITH_LAST, preferred_element_type=jnp.float32
    )
    scores = scores.reshape(conts, slots, 2 * rows)
    lane = lax.broadcasted_iota(jnp.int32, (1, 2 * rows), 1) % rows
    place = lax.broadcasted_iota(jnp.int32, (slots, 2 * rows), 0)
    per_cont = rows // conts
    masked = []
    for c in range(conts):
        limit = jnp.where(lane // per_cont == c, len_ref[c], 0)
        masked.append(jnp.where(place < limit, scores[c], FAR_BELOW))
    scores = jnp.concatenate(masked, axis=0)
    highest = jnp.max(scores, axis=0, keepdims=True)
    weights = jnp.where(
        scores > 0.5 * FAR_BELOW, jnp.exp2((scores - highest) * base_two(head_dim)), 0.0
    )
    totals = jnp.sum(weights, axis=0, keepdims=True)
    numer = lax.dot_general(
        value_ref[...],
        weights.astype(jnp.bfloat16),
        FIRST_WITH_FIRST,
        preferred_element_type=jnp.float32,
    )
    numer_ref[...] = numer.T[:rows]
    stat_ref[...] = jnp.concatenate(
        [highest, totals, jnp.zeros((6, 2 * rows), jnp.float32)], axis=0
    )


def prompt_kernel(query_ref, key_ref, value_hbm, out_ref, value_ref, value_sem):
    blocks, block_rows, head_dim = query_ref.shape
    rows = blocks * block_rows
    copy = pltpu.make_async_copy(value_hbm, value_ref, value_sem)
    copy.start()
    queries = query_ref[...].reshape(rows, head_dim)
    scores = lax.dot_general(
        key_ref[...], queries, LAST_WITH_LAST, preferred_element_type=jnp.float32
    )
    shift = jnp.max(scores, axis=0, keepdims=True).astype(jnp.bfloat16)
    weights = jnp.exp2((scores - shift.astype(jnp.float32)) * base_two(head_dim))
    totals = jnp.sum(weights, axis=0, keepdims=True)
    copy.wait()
    numer = lax.dot_general(
        value_ref[...],
        weights.astype(jnp.bfloat16),
        FIRST_WITH_FIRST,
        preferred_element_type=jnp.float32,
    )
    out_ref[:, :block_rows, :] = (
        numer.T.astype(jnp.bfloat16).reshape(blocks, block_rows, head_dim)
    )
    high = totals.astype(jnp.bfloat16)
    low = totals - high.astype(jnp.float32)
    stats = jnp.concatenate(
        [
            shift.astype(jnp.float32),
            high.astype(jnp.float32),
            low,
            jnp.zeros((STAT_ROWS - 3, rows), jnp.float32),
        ],
        axis=0,
    ).astype(jnp.bfloat16)
    for block in range(blocks):
        tile = block * block_rows // head_dim
        out_ref[block, block_rows:, :] = stats[:, tile * head_dim : (tile + 1) * head_dim]


def combine_kernel(half_ref, back_ref, numer_ref, stat_ref, out_ref, copies_ref, spread_ref, *, rep):
    blocks, _, head_dim = back_ref.shape
    rows = out_ref.shape[0]
    stats = back_ref[:, rows:, :].astype(jnp.float32)
    highs = stats[:, 0, :]
    sums = stats[:, 1, :] + stats[:, 2, :]
    home_high = stat_ref[0:1, :]
    home_sum = stat_ref[1:2, :]
    joint = jnp.maximum(jnp.max(highs, axis=0, keepdims=True), home_high)
    scale = jnp.exp2((highs - joint) * base_two(head_dim))
    home_scale = jnp.exp2((home_high - joint) * base_two(head_dim))
    total = jnp.sum(scale * sums, axis=0, keepdims=True) + home_scale * home_sum
    factors = jnp.concatenate(
        [
            scale / total,
            home_scale / total,
            jnp.zeros((head_dim - blocks - 1, head_dim), jnp.float32),
        ],
        axis=0,
    )
    spread_ref[...] = factors.T
    factors = spread_ref[pl.ds(pl.multiple_of(half_ref[0] * rows, rows), rows), :]
    numer = numer_ref[...] * factors[:, blocks : blocks + 1]
    for block in range(blocks):
        numer += back_ref[block, :rows, :].astype(jnp.float32) * factors[:, block : block + 1]
    out_ref[...] = numer.astype(jnp.bfloat16)
    slabs = numer.reshape(-1, 2, 8, head_dim)
    parts = [
        slabs[:, part].reshape(rows // 2, head_dim).astype(jnp.bfloat16) for part in range(2)
    ]
    for place in range(copies_ref.shape[0]):
        copies_ref[place] = parts[place // rep % 2]


def project_kernel(
    half_ref, block_ref, weight_ref, upper_ref, lower_ref, home_ref, out_ref, home_hbm, wide_ref, home_sem
):
    home_copy = pltpu.make_async_copy(home_ref, home_hbm, home_sem)
    home_copy.start()
    places, block_rows, head_dim = block_ref.shape
    wide_ref[...] = block_ref[...].reshape(places * block_rows, head_dim).astype(jnp.float32)
    heads = weight_ref.shape[0] // (2 * head_dim)
    conts = places * block_rows // heads
    left = jnp.concatenate(
        [
            wide_ref[pl.ds(head, conts, stride=heads), :].astype(jnp.bfloat16)
            for head in range(heads)
        ],
        axis=1,
    )
    half = half_ref[0]
    depth = heads * head_dim
    kept = weight_ref[pl.ds(pl.multiple_of(half * depth, depth), depth), :]
    own = jnp.dot(left, kept, preferred_element_type=jnp.float32).astype(jnp.bfloat16)
    cut = upper_ref.shape[0]
    other = jnp.dot(left[:, :cut], upper_ref[...], preferred_element_type=jnp.float32)
    other += jnp.dot(left[:, cut:], lower_ref[...], preferred_element_type=jnp.float32)
    other = other.astype(jnp.bfloat16)
    out_rows = out_ref.shape[1]
    for group in range(out_ref.shape[0] // 2):
        rows = slice(group * out_rows, (group + 1) * out_rows)
        out_ref[2 * group + half] = own[rows]
        out_ref[2 * group + 1 - half] = other[rows]
    home_copy.wait()


def body(queries, prompt_keys, prompt_values, suffix_keys, suffix_values, suffix_len, out_weight):
    conts, heads, head_dim = queries.shape
    rows = conts * heads
    ctx = lax.axis_size(CTX)
    rep = lax.axis_size(REP)
    kvh = lax.axis_size(KVH)
    half = lax.axis_index("zl")
    tokens = prompt_keys.shape[0]
    slots = suffix_keys.shape[1]
    depth, width = out_weight.shape
    large = pltpu.CompilerParams(vmem_limit_bytes=40 * 2**20)
    small = pltpu.CompilerParams(vmem_limit_bytes=12 * 2**20)
    query_rows = queries.reshape(rows, head_dim)

    with jax.named_scope("gather_queries"):
        copies = jnp.broadcast_to(query_rows[None], (ctx, rows, head_dim))
        visiting = lax.all_to_all(copies, CTX, 0, 0, tiled=False)
    with jax.named_scope("swap_weight"):
        halves = out_weight.reshape(2, depth // 2, width)
        given = lax.dynamic_index_in_dim(halves, 1 - half, 0, keepdims=False)
        cut = depth // 8 * 3
        taken = [
            lax.ppermute(part, "zl", [(0, 1), (1, 0)]) for part in (given[:cut], given[cut:])
        ]
    with jax.named_scope("suffix_attention"):
        home_numer, home_stat = pl.pallas_call(
            functools.partial(suffix_kernel, conts=conts),
            in_specs=[SMEM, VMEM, VMEM, VMEM],
            out_specs=[VMEM, VMEM],
            out_shape=[
                jax.ShapeDtypeStruct((rows, head_dim), jnp.float32),
                jax.ShapeDtypeStruct((8, head_dim), jnp.float32),
            ],
            compiler_params=small,
            cost_estimate=pl.CostEstimate(
                flops=4 * conts * slots * head_dim * head_dim,
                bytes_accessed=4 * conts * slots * head_dim,
                transcendentals=conts * slots * head_dim,
            ),
        )(
            suffix_len,
            query_rows,
            suffix_keys.reshape(conts * slots, head_dim),
            suffix_values.reshape(conts * slots, head_dim),
        )
    visiting, home_numer, home_stat = lax.optimization_barrier(
        (visiting, home_numer, home_stat)
    )
    with jax.named_scope("prompt_attention"):
        sent = pl.pallas_call(
            prompt_kernel,
            in_specs=[VMEM, VMEM, HBM],
            out_specs=VMEM,
            scratch_shapes=[
                pltpu.VMEM((tokens, head_dim), jnp.bfloat16),
                pltpu.SemaphoreType.DMA,
            ],
            out_shape=jax.ShapeDtypeStruct((ctx, rows + STAT_ROWS, head_dim), jnp.bfloat16),
            compiler_params=large,
            cost_estimate=pl.CostEstimate(
                flops=4 * ctx * rows * tokens * head_dim,
                bytes_accessed=4 * tokens * head_dim,
                transcendentals=ctx * rows * tokens,
            ),
        )(
            visiting,
            prompt_keys.reshape(tokens, head_dim),
            pltpu.with_memory_space_constraint(
                prompt_values.reshape(tokens, head_dim), pltpu.HBM
            ),
        )
    sent, taken[0] = lax.optimization_barrier((sent, taken[0]))
    with jax.named_scope("return_partials"):
        back = lax.all_to_all(sent, CTX, 0, 0, tiled=False)
    with jax.named_scope("combine"):
        attended, copies = pl.pallas_call(
            functools.partial(combine_kernel, rep=rep),
            in_specs=[SMEM, VMEM, VMEM, VMEM],
            out_specs=[VMEM, VMEM],
            out_shape=[
                jax.ShapeDtypeStruct((rows, head_dim), jnp.bfloat16),
                jax.ShapeDtypeStruct((ctx * rep, rows // 2, head_dim), jnp.bfloat16),
            ],
            scratch_shapes=[pltpu.VMEM((head_dim, head_dim), jnp.float32)],
            compiler_params=small,
        )(half.reshape(1), back, home_numer, home_stat)
    copies, taken[1] = lax.optimization_barrier((copies, taken[1]))
    with jax.named_scope("gather_attended"):
        everyone = lax.all_to_all(copies, CTX + REP, 0, 0, tiled=False)
    with jax.named_scope("project"):
        terms, attended = pl.pallas_call(
            project_kernel,
            in_specs=[SMEM] + [VMEM] * 5,
            out_specs=[VMEM, HBM],
            out_shape=[
                jax.ShapeDtypeStruct((2 * kvh, ctx * rep * conts // kvh, width), jnp.bfloat16),
                jax.ShapeDtypeStruct((rows, head_dim), jnp.bfloat16),
            ],
            scratch_shapes=[
                pltpu.VMEM((ctx * rep * rows // 2, head_dim), jnp.float32),
                pltpu.SemaphoreType.DMA,
            ],
            compiler_params=small,
        )(half.reshape(1), everyone, out_weight, taken[0], taken[1], attended)
    with jax.named_scope("sum_heads"):
        parts = lax.all_to_all(terms, KVH + ("zl",), 0, 0, tiled=False)
        projected = jnp.sum(parts.astype(jnp.float32), axis=0).astype(jnp.bfloat16)
    return (attended.reshape(conts, heads, head_dim), projected)


def solution(mesh):
    ctx, kvh, rep = (mesh.shape[name] for name in ("ctx", "kvh", "rep"))
    fine = Mesh(
        mesh.devices.reshape(ctx // 2, 2, kvh // 2, 2, rep), ("y", "zl", "x", "core", "zh")
    )
    groups = CTX + REP
    in_specs = (
        P(groups, KVH, None),
        P(CTX, KVH, None),
        P(CTX, KVH, None),
        P(groups, None, KVH, None),
        P(groups, None, KVH, None),
        P(groups),
        P(KVH, groups),
    )
    out_specs = (P(groups, KVH, None), P(KVH, groups))
    return jax.shard_map(body, mesh=fine, in_specs=in_specs, out_specs=out_specs, check_vma=False)
```

```python
import functools
import math

import jax
import jax.numpy as jnp
import numpy as np
from jax import lax
from jax.experimental import pallas as pl
from jax.experimental.pallas import tpu as pltpu
from jax.sharding import Mesh
from jax.sharding import PartitionSpec as P

FAR_BELOW = -1e30
CTX = ("y4", "y2", "y1", "zl")
KVH = ("x", "core")
REP = ("z4", "z2")
CTX_ORDER = ("zl", "y4", "y1", "y2")
ALL_ORDER = ("y4", "y2", "y1", "z4", "z2", "zl")
VMEM = pl.BlockSpec(memory_space=pltpu.VMEM)
HBM = pl.BlockSpec(memory_space=pltpu.HBM)
SMEM = pl.BlockSpec(memory_space=pltpu.SMEM)
LAST_WITH_LAST = (((1,), (1,)), ((), ()))
FIRST_WITH_FIRST = (((0,), (0,)), ((), ()))
STAT_ROWS = 8


def home_places(sizes):
    names = CTX + REP
    grid = np.arange(math.prod(sizes)).reshape(sizes)
    return grid.transpose([names.index(name) for name in ALL_ORDER]).reshape(-1).tolist()


def base_two(head_dim):
    return math.log2(math.e) / math.sqrt(head_dim)


def suffix_kernel(len_ref, query_ref, key_ref, value_ref, numer_ref, stat_ref, *, conts):
    rows, head_dim = query_ref.shape
    slots = key_ref.shape[0] // conts
    twice = jnp.concatenate([query_ref[...]] * 2, axis=0)
    scores = lax.dot_general(
        key_ref[...], twice, LAST_WITH_LAST, preferred_element_type=jnp.float32
    )
    scores = scores.reshape(conts, slots, 2 * rows)
    lane = lax.broadcasted_iota(jnp.int32, (1, 2 * rows), 1) % rows
    place = lax.broadcasted_iota(jnp.int32, (slots, 2 * rows), 0)
    per_cont = rows // conts
    masked = []
    for c in range(conts):
        limit = jnp.where(lane // per_cont == c, len_ref[c], 0)
        masked.append(jnp.where(place < limit, scores[c], FAR_BELOW))
    scores = jnp.concatenate(masked, axis=0)
    highest = jnp.max(scores, axis=0, keepdims=True)
    weights = jnp.where(
        scores > 0.5 * FAR_BELOW, jnp.exp2((scores - highest) * base_two(head_dim)), 0.0
    )
    totals = jnp.sum(weights, axis=0, keepdims=True)
    numer = lax.dot_general(
        value_ref[...],
        weights.astype(jnp.bfloat16),
        FIRST_WITH_FIRST,
        preferred_element_type=jnp.float32,
    )
    numer_ref[...] = numer.T[:rows]
    stat_ref[...] = jnp.concatenate(
        [highest, totals, jnp.zeros((6, 2 * rows), jnp.float32)], axis=0
    )


def prompt_kernel(query_ref, key_ref, value_hbm, out_ref, value_ref, value_sem):
    blocks, block_rows, head_dim = query_ref.shape
    rows = blocks * block_rows
    copy = pltpu.make_async_copy(value_hbm, value_ref, value_sem)
    copy.start()
    queries = query_ref[...].reshape(rows, head_dim)
    scores = lax.dot_general(
        key_ref[...], queries, LAST_WITH_LAST, preferred_element_type=jnp.float32
    )
    shift = jnp.max(scores, axis=0, keepdims=True).astype(jnp.bfloat16)
    weights = jnp.exp2((scores - shift.astype(jnp.float32)) * base_two(head_dim))
    totals = jnp.sum(weights, axis=0, keepdims=True)
    copy.wait()
    numer = lax.dot_general(
        value_ref[...],
        weights.astype(jnp.bfloat16),
        FIRST_WITH_FIRST,
        preferred_element_type=jnp.float32,
    )
    out_ref[:, :block_rows, :] = (
        numer.T.astype(jnp.bfloat16).reshape(blocks, block_rows, head_dim)
    )
    high = totals.astype(jnp.bfloat16)
    low = totals - high.astype(jnp.float32)
    stats = jnp.concatenate(
        [
            shift.astype(jnp.float32),
            high.astype(jnp.float32),
            low,
            jnp.zeros((STAT_ROWS - 3, rows), jnp.float32),
        ],
        axis=0,
    ).astype(jnp.bfloat16)
    for block in range(blocks):
        tile = block * block_rows // head_dim
        out_ref[block, block_rows:, :] = stats[:, tile * head_dim : (tile + 1) * head_dim]


def combine_kernel(
    half_ref, back_ref, numer_ref, stat_ref, out_ref, copies_ref, spread_ref, *, sides
):
    blocks, _, head_dim = back_ref.shape
    rows = out_ref.shape[0]
    stats = back_ref[:, rows:, :].astype(jnp.float32)
    highs = stats[:, 0, :]
    sums = stats[:, 1, :] + stats[:, 2, :]
    home_high = stat_ref[0:1, :]
    home_sum = stat_ref[1:2, :]
    joint = jnp.maximum(jnp.max(highs, axis=0, keepdims=True), home_high)
    scale = jnp.exp2((highs - joint) * base_two(head_dim))
    home_scale = jnp.exp2((home_high - joint) * base_two(head_dim))
    total = jnp.sum(scale * sums, axis=0, keepdims=True) + home_scale * home_sum
    factors = jnp.concatenate(
        [
            scale / total,
            home_scale / total,
            jnp.zeros((head_dim - blocks - 1, head_dim), jnp.float32),
        ],
        axis=0,
    )
    spread_ref[...] = factors.T
    factors = spread_ref[pl.ds(pl.multiple_of(half_ref[0] * rows, rows), rows), :]
    numer = numer_ref[...] * factors[:, blocks : blocks + 1]
    for block in range(blocks):
        numer += back_ref[block, :rows, :].astype(jnp.float32) * factors[:, block : block + 1]
    out_ref[...] = numer.astype(jnp.bfloat16)
    slabs = numer.reshape(-1, 2, 8, head_dim)
    parts = [
        slabs[:, part].reshape(rows // 2, head_dim).astype(jnp.bfloat16) for part in range(2)
    ]
    for place, side in enumerate(sides):
        copies_ref[place] = parts[side]


def project_kernel(
    half_ref,
    block_ref,
    weight_ref,
    upper_ref,
    lower_ref,
    home_ref,
    out_ref,
    home_hbm,
    wide_ref,
    home_sem,
    *,
    homes,
):
    home_copy = pltpu.make_async_copy(home_ref, home_hbm, home_sem)
    home_copy.start()
    places, block_rows, head_dim = block_ref.shape
    for place, home in enumerate(homes):
        wide_ref[pl.ds(home * block_rows, block_rows), :] = block_ref[place].astype(jnp.float32)
    heads = weight_ref.shape[0] // (2 * head_dim)
    conts = places * block_rows // heads
    left = jnp.concatenate(
        [
            wide_ref[pl.ds(head, conts, stride=heads), :].astype(jnp.bfloat16)
            for head in range(heads)
        ],
        axis=1,
    )
    half = half_ref[0]
    depth = heads * head_dim
    kept = weight_ref[pl.ds(pl.multiple_of(half * depth, depth), depth), :]
    own = jnp.dot(left, kept, preferred_element_type=jnp.float32).astype(jnp.bfloat16)
    cut = upper_ref.shape[0]
    other = jnp.dot(left[:, :cut], upper_ref[...], preferred_element_type=jnp.float32)
    other += jnp.dot(left[:, cut:], lower_ref[...], preferred_element_type=jnp.float32)
    other = other.astype(jnp.bfloat16)
    out_rows = out_ref.shape[1]
    for group in range(out_ref.shape[0] // 2):
        rows = slice(group * out_rows, (group + 1) * out_rows)
        out_ref[2 * group + half] = own[rows]
        out_ref[2 * group + 1 - half] = other[rows]
    home_copy.wait()


def body(queries, prompt_keys, prompt_values, suffix_keys, suffix_values, suffix_len, out_weight):
    conts, heads, head_dim = queries.shape
    rows = conts * heads
    ctx = lax.axis_size(CTX)
    rep = lax.axis_size(REP)
    kvh = lax.axis_size(KVH)
    half = lax.axis_index("zl")
    homes = home_places([lax.axis_size(name) for name in CTX + REP])
    tokens = prompt_keys.shape[0]
    slots = suffix_keys.shape[1]
    depth, width = out_weight.shape
    large = pltpu.CompilerParams(vmem_limit_bytes=40 * 2**20)
    small = pltpu.CompilerParams(vmem_limit_bytes=12 * 2**20)
    query_rows = queries.reshape(rows, head_dim)

    with jax.named_scope("gather_queries"):
        copies = jnp.broadcast_to(query_rows[None], (ctx, rows, head_dim))
        visiting = lax.all_to_all(copies, CTX_ORDER, 0, 0, tiled=False)
    with jax.named_scope("swap_weight"):
        halves = out_weight.reshape(2, depth // 2, width)
        given = lax.dynamic_index_in_dim(halves, 1 - half, 0, keepdims=False)
        cut = depth // 8 * 3
        taken = [
            lax.ppermute(part, "zl", [(0, 1), (1, 0)]) for part in (given[:cut], given[cut:])
        ]
    with jax.named_scope("suffix_attention"):
        home_numer, home_stat = pl.pallas_call(
            functools.partial(suffix_kernel, conts=conts),
            in_specs=[SMEM, VMEM, VMEM, VMEM],
            out_specs=[VMEM, VMEM],
            out_shape=[
                jax.ShapeDtypeStruct((rows, head_dim), jnp.float32),
                jax.ShapeDtypeStruct((8, head_dim), jnp.float32),
            ],
            compiler_params=small,
            cost_estimate=pl.CostEstimate(
                flops=4 * conts * slots * head_dim * head_dim,
                bytes_accessed=4 * conts * slots * head_dim,
                transcendentals=conts * slots * head_dim,
            ),
        )(
            suffix_len,
            query_rows,
            suffix_keys.reshape(conts * slots, head_dim),
            suffix_values.reshape(conts * slots, head_dim),
        )
    visiting, home_numer, home_stat = lax.optimization_barrier(
        (visiting, home_numer, home_stat)
    )
    with jax.named_scope("prompt_attention"):
        sent = pl.pallas_call(
            prompt_kernel,
            in_specs=[VMEM, VMEM, HBM],
            out_specs=VMEM,
            scratch_shapes=[
                pltpu.VMEM((tokens, head_dim), jnp.bfloat16),
                pltpu.SemaphoreType.DMA,
            ],
            out_shape=jax.ShapeDtypeStruct((ctx, rows + STAT_ROWS, head_dim), jnp.bfloat16),
            compiler_params=large,
            cost_estimate=pl.CostEstimate(
                flops=4 * ctx * rows * tokens * head_dim,
                bytes_accessed=4 * tokens * head_dim,
                transcendentals=ctx * rows * tokens,
            ),
        )(
            visiting,
            prompt_keys.reshape(tokens, head_dim),
            pltpu.with_memory_space_constraint(
                prompt_values.reshape(tokens, head_dim), pltpu.HBM
            ),
        )
    sent, taken[0] = lax.optimization_barrier((sent, taken[0]))
    with jax.named_scope("return_partials"):
        back = lax.all_to_all(sent, CTX_ORDER, 0, 0, tiled=False)
    with jax.named_scope("combine"):
        attended, copies = pl.pallas_call(
            functools.partial(combine_kernel, sides=[home // rep % 2 for home in homes]),
            in_specs=[SMEM, VMEM, VMEM, VMEM],
            out_specs=[VMEM, VMEM],
            out_shape=[
                jax.ShapeDtypeStruct((rows, head_dim), jnp.bfloat16),
                jax.ShapeDtypeStruct((ctx * rep, rows // 2, head_dim), jnp.bfloat16),
            ],
            scratch_shapes=[pltpu.VMEM((head_dim, head_dim), jnp.float32)],
            compiler_params=small,
        )(lax.axis_index(CTX_ORDER[-1]).reshape(1), back, home_numer, home_stat)
    copies, taken[1] = lax.optimization_barrier((copies, taken[1]))
    with jax.named_scope("gather_attended"):
        everyone = lax.all_to_all(copies, ALL_ORDER, 0, 0, tiled=False)
    with jax.named_scope("project"):
        terms, attended = pl.pallas_call(
            functools.partial(project_kernel, homes=homes),
            in_specs=[SMEM] + [VMEM] * 5,
            out_specs=[VMEM, HBM],
            out_shape=[
                jax.ShapeDtypeStruct((2 * kvh, ctx * rep * conts // kvh, width), jnp.bfloat16),
                jax.ShapeDtypeStruct((rows, head_dim), jnp.bfloat16),
            ],
            scratch_shapes=[
                pltpu.VMEM((ctx * rep * rows // 2, head_dim), jnp.float32),
                pltpu.SemaphoreType.DMA,
            ],
            compiler_params=small,
        )(half.reshape(1), everyone, out_weight, taken[0], taken[1], attended)
    with jax.named_scope("sum_heads"):
        parts = lax.all_to_all(terms, KVH + ("zl",), 0, 0, tiled=False)
        projected = jnp.sum(parts.astype(jnp.float32), axis=0).astype(jnp.bfloat16)
    return (attended.reshape(conts, heads, head_dim), projected)


def solution(mesh):
    ctx, kvh, rep = (mesh.shape[name] for name in ("ctx", "kvh", "rep"))
    fine = Mesh(
        mesh.devices.reshape(2, 2, ctx // 8, 2, kvh // 2, 2, 2, rep // 2),
        CTX + KVH + REP,
    )
    groups = CTX + REP
    in_specs = (
        P(groups, KVH, None),
        P(CTX, KVH, None),
        P(CTX, KVH, None),
        P(groups, None, KVH, None),
        P(groups, None, KVH, None),
        P(groups),
        P(KVH, groups),
    )
    out_specs = (P(groups, KVH, None), P(KVH, groups))
    return jax.shard_map(body, mesh=fine, in_specs=in_specs, out_specs=out_specs, check_vma=False)
```

```python
import functools
import math

import jax
import jax.numpy as jnp
import numpy as np
from jax import lax
from jax.experimental import pallas as pl
from jax.experimental.pallas import tpu as pltpu
from jax.sharding import Mesh
from jax.sharding import PartitionSpec as P

FAR_BELOW = -1e30
CTX = ("y4", "y2", "y1", "zl")
KVH = ("x", "core")
REP = ("z4", "z2")
CTX_ORDER = ("zl", "y4", "y1", "y2")
ALL_ORDER = ("y4", "y1", "y2", "z4", "z2", "zl")
VMEM = pl.BlockSpec(memory_space=pltpu.VMEM)
HBM = pl.BlockSpec(memory_space=pltpu.HBM)
SMEM = pl.BlockSpec(memory_space=pltpu.SMEM)
LAST_WITH_LAST = (((1,), (1,)), ((), ()))
FIRST_WITH_FIRST = (((0,), (0,)), ((), ()))
STAT_ROWS = 8


def home_places(sizes):
    names = CTX + REP
    grid = np.arange(math.prod(sizes)).reshape(sizes)
    return grid.transpose([names.index(name) for name in ALL_ORDER]).reshape(-1).tolist()


def base_two(head_dim):
    return math.log2(math.e) / math.sqrt(head_dim)


def suffix_kernel(len_ref, query_ref, key_ref, value_ref, numer_ref, stat_ref, *, conts):
    rows, head_dim = query_ref.shape
    slots = key_ref.shape[0] // conts
    twice = jnp.concatenate([query_ref[...]] * 2, axis=0)
    scores = lax.dot_general(
        key_ref[...], twice, LAST_WITH_LAST, preferred_element_type=jnp.float32
    )
    scores = scores.reshape(conts, slots, 2 * rows)
    lane = lax.broadcasted_iota(jnp.int32, (1, 2 * rows), 1) % rows
    place = lax.broadcasted_iota(jnp.int32, (slots, 2 * rows), 0)
    per_cont = rows // conts
    masked = []
    for c in range(conts):
        limit = jnp.where(lane // per_cont == c, len_ref[c], 0)
        masked.append(jnp.where(place < limit, scores[c], FAR_BELOW))
    scores = jnp.concatenate(masked, axis=0)
    highest = jnp.max(scores, axis=0, keepdims=True)
    weights = jnp.where(
        scores > 0.5 * FAR_BELOW, jnp.exp2((scores - highest) * base_two(head_dim)), 0.0
    )
    totals = jnp.sum(weights, axis=0, keepdims=True)
    numer = lax.dot_general(
        value_ref[...],
        weights.astype(jnp.bfloat16),
        FIRST_WITH_FIRST,
        preferred_element_type=jnp.float32,
    )
    numer_ref[...] = numer.T[:rows]
    stat_ref[...] = jnp.concatenate(
        [highest, totals, jnp.zeros((6, 2 * rows), jnp.float32)], axis=0
    )


def prompt_kernel(query_ref, key_ref, value_hbm, out_ref, value_ref, value_sem):
    blocks, block_rows, head_dim = query_ref.shape
    rows = blocks * block_rows
    copy = pltpu.make_async_copy(value_hbm, value_ref, value_sem)
    copy.start()
    queries = query_ref[...].reshape(rows, head_dim)
    scores = lax.dot_general(
        key_ref[...], queries, LAST_WITH_LAST, preferred_element_type=jnp.float32
    )
    shift = jnp.max(scores, axis=0, keepdims=True).astype(jnp.bfloat16)
    weights = jnp.exp2((scores - shift.astype(jnp.float32)) * base_two(head_dim))
    totals = jnp.sum(weights, axis=0, keepdims=True)
    copy.wait()
    numer = lax.dot_general(
        value_ref[...],
        weights.astype(jnp.bfloat16),
        FIRST_WITH_FIRST,
        preferred_element_type=jnp.float32,
    )
    out_ref[:, :block_rows, :] = (
        numer.T.astype(jnp.bfloat16).reshape(blocks, block_rows, head_dim)
    )
    high = totals.astype(jnp.bfloat16)
    low = totals - high.astype(jnp.float32)
    stats = jnp.concatenate(
        [
            shift.astype(jnp.float32),
            high.astype(jnp.float32),
            low,
            jnp.zeros((STAT_ROWS - 3, rows), jnp.float32),
        ],
        axis=0,
    ).astype(jnp.bfloat16)
    for block in range(blocks):
        tile = block * block_rows // head_dim
        out_ref[block, block_rows:, :] = stats[:, tile * head_dim : (tile + 1) * head_dim]


def combine_kernel(
    half_ref, back_ref, numer_ref, stat_ref, out_ref, copies_ref, spread_ref, *, sides
):
    blocks, _, head_dim = back_ref.shape
    rows = out_ref.shape[0]
    stats = back_ref[:, rows:, :].astype(jnp.float32)
    highs = stats[:, 0, :]
    sums = stats[:, 1, :] + stats[:, 2, :]
    home_high = stat_ref[0:1, :]
    home_sum = stat_ref[1:2, :]
    joint = jnp.maximum(jnp.max(highs, axis=0, keepdims=True), home_high)
    scale = jnp.exp2((highs - joint) * base_two(head_dim))
    home_scale = jnp.exp2((home_high - joint) * base_two(head_dim))
    total = jnp.sum(scale * sums, axis=0, keepdims=True) + home_scale * home_sum
    factors = jnp.concatenate(
        [
            scale / total,
            home_scale / total,
            jnp.zeros((head_dim - blocks - 1, head_dim), jnp.float32),
        ],
        axis=0,
    )
    spread_ref[...] = factors.T
    factors = spread_ref[pl.ds(pl.multiple_of(half_ref[0] * rows, rows), rows), :]
    numer = numer_ref[...] * factors[:, blocks : blocks + 1]
    for block in range(blocks):
        numer += back_ref[block, :rows, :].astype(jnp.float32) * factors[:, block : block + 1]
    out_ref[...] = numer.astype(jnp.bfloat16)
    slabs = numer.reshape(-1, 2, 8, head_dim)
    parts = [
        slabs[:, part].reshape(rows // 2, head_dim).astype(jnp.bfloat16) for part in range(2)
    ]
    for place, side in enumerate(sides):
        copies_ref[place] = parts[side]


def project_kernel(
    half_ref,
    block_ref,
    weight_ref,
    upper_ref,
    lower_ref,
    home_ref,
    out_ref,
    home_hbm,
    wide_ref,
    home_sem,
    *,
    homes,
):
    home_copy = pltpu.make_async_copy(home_ref, home_hbm, home_sem)
    home_copy.start()
    places, block_rows, head_dim = block_ref.shape
    for place, home in enumerate(homes):
        wide_ref[pl.ds(home * block_rows, block_rows), :] = block_ref[place].astype(jnp.float32)
    heads = weight_ref.shape[0] // (2 * head_dim)
    conts = places * block_rows // heads
    left = jnp.concatenate(
        [
            wide_ref[pl.ds(head, conts, stride=heads), :].astype(jnp.bfloat16)
            for head in range(heads)
        ],
        axis=1,
    )
    half = half_ref[0]
    depth = heads * head_dim
    kept = weight_ref[pl.ds(pl.multiple_of(half * depth, depth), depth), :]
    own = jnp.dot(left, kept, preferred_element_type=jnp.float32).astype(jnp.bfloat16)
    cut = upper_ref.shape[0]
    other = jnp.dot(left[:, :cut], upper_ref[...], preferred_element_type=jnp.float32)
    other += jnp.dot(left[:, cut:], lower_ref[...], preferred_element_type=jnp.float32)
    other = other.astype(jnp.bfloat16)
    out_rows = out_ref.shape[1]
    for group in range(out_ref.shape[0] // 2):
        rows = slice(group * out_rows, (group + 1) * out_rows)
        out_ref[2 * group + half] = own[rows]
        out_ref[2 * group + 1 - half] = other[rows]
    home_copy.wait()


def body(queries, prompt_keys, prompt_values, suffix_keys, suffix_values, suffix_len, out_weight):
    conts, heads, head_dim = queries.shape
    rows = conts * heads
    ctx = lax.axis_size(CTX)
    rep = lax.axis_size(REP)
    kvh = lax.axis_size(KVH)
    half = lax.axis_index("zl")
    homes = home_places([lax.axis_size(name) for name in CTX + REP])
    tokens = prompt_keys.shape[0]
    slots = suffix_keys.shape[1]
    depth, width = out_weight.shape
    large = pltpu.CompilerParams(vmem_limit_bytes=40 * 2**20)
    small = pltpu.CompilerParams(vmem_limit_bytes=12 * 2**20)
    query_rows = queries.reshape(rows, head_dim)

    with jax.named_scope("gather_queries"):
        copies = jnp.broadcast_to(query_rows[None], (ctx, rows, head_dim))
        visiting = lax.all_to_all(copies, CTX_ORDER, 0, 0, tiled=False)
    with jax.named_scope("swap_weight"):
        halves = out_weight.reshape(2, depth // 2, width)
        given = lax.dynamic_index_in_dim(halves, 1 - half, 0, keepdims=False)
        cut = depth // 8 * 3
        taken = [
            lax.ppermute(part, "zl", [(0, 1), (1, 0)]) for part in (given[:cut], given[cut:])
        ]
    with jax.named_scope("suffix_attention"):
        home_numer, home_stat = pl.pallas_call(
            functools.partial(suffix_kernel, conts=conts),
            in_specs=[SMEM, VMEM, VMEM, VMEM],
            out_specs=[VMEM, VMEM],
            out_shape=[
                jax.ShapeDtypeStruct((rows, head_dim), jnp.float32),
                jax.ShapeDtypeStruct((8, head_dim), jnp.float32),
            ],
            compiler_params=small,
            cost_estimate=pl.CostEstimate(
                flops=4 * conts * slots * head_dim * head_dim,
                bytes_accessed=4 * conts * slots * head_dim,
                transcendentals=conts * slots * head_dim,
            ),
        )(
            pltpu.with_memory_space_constraint(suffix_len, pltpu.HBM),
            query_rows,
            suffix_keys.reshape(conts * slots, head_dim),
            suffix_values.reshape(conts * slots, head_dim),
        )
    visiting, home_numer, home_stat = lax.optimization_barrier(
        (visiting, home_numer, home_stat)
    )
    with jax.named_scope("prompt_attention"):
        sent = pl.pallas_call(
            prompt_kernel,
            in_specs=[VMEM, VMEM, HBM],
            out_specs=VMEM,
            scratch_shapes=[
                pltpu.VMEM((tokens, head_dim), jnp.bfloat16),
                pltpu.SemaphoreType.DMA,
            ],
            out_shape=jax.ShapeDtypeStruct((ctx, rows + STAT_ROWS, head_dim), jnp.bfloat16),
            compiler_params=large,
            cost_estimate=pl.CostEstimate(
                flops=4 * ctx * rows * tokens * head_dim,
                bytes_accessed=4 * tokens * head_dim,
                transcendentals=ctx * rows * tokens,
            ),
        )(
            visiting,
            prompt_keys.reshape(tokens, head_dim),
            pltpu.with_memory_space_constraint(
                prompt_values.reshape(tokens, head_dim), pltpu.HBM
            ),
        )
    sent, taken[0] = lax.optimization_barrier((sent, taken[0]))
    with jax.named_scope("return_partials"):
        back = lax.all_to_all(sent, CTX_ORDER, 0, 0, tiled=False)
    with jax.named_scope("combine"):
        attended, copies = pl.pallas_call(
            functools.partial(combine_kernel, sides=[home // rep % 2 for home in homes]),
            in_specs=[SMEM, VMEM, VMEM, VMEM],
            out_specs=[VMEM, VMEM],
            out_shape=[
                jax.ShapeDtypeStruct((rows, head_dim), jnp.bfloat16),
                jax.ShapeDtypeStruct((ctx * rep, rows // 2, head_dim), jnp.bfloat16),
            ],
            scratch_shapes=[pltpu.VMEM((head_dim, head_dim), jnp.float32)],
            compiler_params=small,
        )(lax.axis_index(CTX_ORDER[-1]).reshape(1), back, home_numer, home_stat)
    copies, taken[1] = lax.optimization_barrier((copies, taken[1]))
    with jax.named_scope("gather_attended"):
        everyone = lax.all_to_all(copies, ALL_ORDER, 0, 0, tiled=False)
    with jax.named_scope("project"):
        terms, attended = pl.pallas_call(
            functools.partial(project_kernel, homes=homes),
            in_specs=[SMEM] + [VMEM] * 5,
            out_specs=[VMEM, HBM],
            out_shape=[
                jax.ShapeDtypeStruct((2 * kvh, ctx * rep * conts // kvh, width), jnp.bfloat16),
                jax.ShapeDtypeStruct((rows, head_dim), jnp.bfloat16),
            ],
            scratch_shapes=[
                pltpu.VMEM((ctx * rep * rows // 2, head_dim), jnp.float32),
                pltpu.SemaphoreType.DMA,
            ],
            compiler_params=small,
        )(half.reshape(1), everyone, out_weight, taken[0], taken[1], attended)
    with jax.named_scope("sum_heads"):
        parts = lax.all_to_all(terms, KVH + ("zl",), 0, 0, tiled=False)
        projected = jnp.sum(parts.astype(jnp.float32), axis=0).astype(jnp.bfloat16)
    return (attended.reshape(conts, heads, head_dim), projected)


def solution(mesh):
    ctx, kvh, rep = (mesh.shape[name] for name in ("ctx", "kvh", "rep"))
    fine = Mesh(
        mesh.devices.reshape(2, 2, ctx // 8, 2, kvh // 2, 2, 2, rep // 2),
        CTX + KVH + REP,
    )
    groups = CTX + REP
    in_specs = (
        P(groups, KVH, None),
        P(CTX, KVH, None),
        P(CTX, KVH, None),
        P(groups, None, KVH, None),
        P(groups, None, KVH, None),
        P(groups),
        P(KVH, groups),
    )
    out_specs = (P(groups, KVH, None), P(KVH, groups))
    return jax.shard_map(body, mesh=fine, in_specs=in_specs, out_specs=out_specs, check_vma=False)
```

```python
import functools
import math

import jax
import jax.numpy as jnp
import numpy as np
from jax import lax
from jax.experimental import pallas as pl
from jax.experimental.pallas import tpu as pltpu
from jax.sharding import Mesh
from jax.sharding import PartitionSpec as P

FAR_BELOW = -1e30
CTX = ("y4", "y2", "y1", "zl")
KVH = ("x", "core")
REP = ("z4", "z2")
CTX_ORDER = ("zl", "y4", "y1", "y2")
ALL_ORDER = ("y4", "y2", "y1", "z4", "z2", "zl")
VMEM = pl.BlockSpec(memory_space=pltpu.VMEM)
HBM = pl.BlockSpec(memory_space=pltpu.HBM)
SMEM = pl.BlockSpec(memory_space=pltpu.SMEM)
LAST_WITH_LAST = (((1,), (1,)), ((), ()))
FIRST_WITH_FIRST = (((0,), (0,)), ((), ()))
STAT_ROWS = 8


def home_places(sizes):
    names = CTX + REP
    grid = np.arange(math.prod(sizes)).reshape(sizes)
    return grid.transpose([names.index(name) for name in ALL_ORDER]).reshape(-1).tolist()


def base_two(head_dim):
    return math.log2(math.e) / math.sqrt(head_dim)


def suffix_kernel(len_ref, query_ref, key_ref, value_ref, numer_ref, stat_ref, *, conts):
    rows, head_dim = query_ref.shape
    slots = key_ref.shape[0] // conts
    twice = jnp.concatenate([query_ref[...]] * 2, axis=0)
    scores = lax.dot_general(
        key_ref[...], twice, LAST_WITH_LAST, preferred_element_type=jnp.float32
    )
    scores = scores.reshape(conts, slots, 2 * rows)
    lane = lax.broadcasted_iota(jnp.int32, (1, 2 * rows), 1) % rows
    place = lax.broadcasted_iota(jnp.int32, (slots, 2 * rows), 0)
    per_cont = rows // conts
    masked = []
    for c in range(conts):
        limit = jnp.where(lane // per_cont == c, len_ref[c], 0)
        masked.append(jnp.where(place < limit, scores[c], FAR_BELOW))
    scores = jnp.concatenate(masked, axis=0)
    highest = jnp.max(scores, axis=0, keepdims=True)
    weights = jnp.where(
        scores > 0.5 * FAR_BELOW, jnp.exp2((scores - highest) * base_two(head_dim)), 0.0
    )
    totals = jnp.sum(weights, axis=0, keepdims=True)
    numer = lax.dot_general(
        value_ref[...],
        weights.astype(jnp.bfloat16),
        FIRST_WITH_FIRST,
        preferred_element_type=jnp.float32,
    )
    numer_ref[...] = numer.T[:rows]
    stat_ref[...] = jnp.concatenate(
        [highest, totals, jnp.zeros((6, 2 * rows), jnp.float32)], axis=0
    )


def prompt_kernel(query_ref, key_ref, value_hbm, out_ref, value_ref, value_sem):
    blocks, block_rows, head_dim = query_ref.shape
    rows = blocks * block_rows
    copy = pltpu.make_async_copy(value_hbm, value_ref, value_sem)
    copy.start()
    queries = query_ref[...].reshape(rows, head_dim)
    scores = lax.dot_general(
        key_ref[...], queries, LAST_WITH_LAST, preferred_element_type=jnp.float32
    )
    shift = jnp.max(scores, axis=0, keepdims=True).astype(jnp.bfloat16)
    weights = jnp.exp2((scores - shift.astype(jnp.float32)) * base_two(head_dim))
    totals = jnp.sum(weights, axis=0, keepdims=True)
    copy.wait()
    numer = lax.dot_general(
        value_ref[...],
        weights.astype(jnp.bfloat16),
        FIRST_WITH_FIRST,
        preferred_element_type=jnp.float32,
    )
    out_ref[:, :block_rows, :] = (
        numer.T.astype(jnp.bfloat16).reshape(blocks, block_rows, head_dim)
    )
    high = totals.astype(jnp.bfloat16)
    low = totals - high.astype(jnp.float32)
    stats = jnp.concatenate(
        [
            shift.astype(jnp.float32),
            high.astype(jnp.float32),
            low,
            jnp.zeros((STAT_ROWS - 3, rows), jnp.float32),
        ],
        axis=0,
    ).astype(jnp.bfloat16)
    for block in range(blocks):
        tile = block * block_rows // head_dim
        out_ref[block, block_rows:, :] = stats[:, tile * head_dim : (tile + 1) * head_dim]


def combine_kernel(
    half_ref, back_ref, numer_ref, stat_ref, out_ref, copies_ref, spread_ref, *, sides
):
    blocks, _, head_dim = back_ref.shape
    rows = out_ref.shape[0]
    stats = back_ref[:, rows:, :].astype(jnp.float32)
    highs = stats[:, 0, :]
    sums = stats[:, 1, :] + stats[:, 2, :]
    home_high = stat_ref[0:1, :]
    home_sum = stat_ref[1:2, :]
    joint = jnp.maximum(jnp.max(highs, axis=0, keepdims=True), home_high)
    scale = jnp.exp2((highs - joint) * base_two(head_dim))
    home_scale = jnp.exp2((home_high - joint) * base_two(head_dim))
    total = jnp.sum(scale * sums, axis=0, keepdims=True) + home_scale * home_sum
    factors = jnp.concatenate(
        [
            scale / total,
            home_scale / total,
            jnp.zeros((head_dim - blocks - 1, head_dim), jnp.float32),
        ],
        axis=0,
    )
    spread_ref[...] = factors.T
    factors = spread_ref[pl.ds(pl.multiple_of(half_ref[0] * rows, rows), rows), :]
    numer = numer_ref[...] * factors[:, blocks : blocks + 1]
    for block in range(blocks):
        numer += back_ref[block, :rows, :].astype(jnp.float32) * factors[:, block : block + 1]
    out_ref[...] = numer.astype(jnp.bfloat16)
    slabs = numer.reshape(-1, 2, 8, head_dim)
    parts = [
        slabs[:, part].reshape(rows // 2, head_dim).astype(jnp.bfloat16) for part in range(2)
    ]
    for place, side in enumerate(sides):
        copies_ref[place] = parts[side]


def project_kernel(
    half_ref,
    block_ref,
    weight_ref,
    upper_ref,
    lower_ref,
    home_ref,
    out_ref,
    home_hbm,
    wide_ref,
    home_sem,
    *,
    homes,
):
    home_copy = pltpu.make_async_copy(home_ref, home_hbm, home_sem)
    home_copy.start()
    places, block_rows, head_dim = block_ref.shape
    for place, home in enumerate(homes):
        wide_ref[pl.ds(home * block_rows, block_rows), :] = block_ref[place].astype(jnp.float32)
    heads = weight_ref.shape[0] // (2 * head_dim)
    conts = places * block_rows // heads
    left = jnp.concatenate(
        [
            wide_ref[pl.ds(head, conts, stride=heads), :].astype(jnp.bfloat16)
            for head in range(heads)
        ],
        axis=1,
    )
    half = half_ref[0]
    depth = heads * head_dim
    kept = weight_ref[pl.ds(pl.multiple_of(half * depth, depth), depth), :]
    own = jnp.dot(left, kept, preferred_element_type=jnp.float32).astype(jnp.bfloat16)
    cut = upper_ref.shape[0]
    other = jnp.dot(left[:, :cut], upper_ref[...], preferred_element_type=jnp.float32)
    other += jnp.dot(left[:, cut:], lower_ref[...], preferred_element_type=jnp.float32)
    other = other.astype(jnp.bfloat16)
    out_rows = out_ref.shape[1]
    for group in range(out_ref.shape[0] // 2):
        rows = slice(group * out_rows, (group + 1) * out_rows)
        out_ref[2 * group + half] = own[rows]
        out_ref[2 * group + 1 - half] = other[rows]
    home_copy.wait()


def sum_kernel(part_ref, out_ref):
    total = part_ref[0].astype(jnp.float32)
    for part in range(1, part_ref.shape[0]):
        total += part_ref[part].astype(jnp.float32)
    out_ref[...] = total.astype(out_ref.dtype)


def body(queries, prompt_keys, prompt_values, suffix_keys, suffix_values, suffix_len, out_weight):
    conts, heads, head_dim = queries.shape
    rows = conts * heads
    ctx = lax.axis_size(CTX)
    rep = lax.axis_size(REP)
    kvh = lax.axis_size(KVH)
    half = lax.axis_index("zl")
    homes = home_places([lax.axis_size(name) for name in CTX + REP])
    tokens = prompt_keys.shape[0]
    slots = suffix_keys.shape[1]
    depth, width = out_weight.shape
    large = pltpu.CompilerParams(vmem_limit_bytes=40 * 2**20)
    small = pltpu.CompilerParams(vmem_limit_bytes=12 * 2**20)
    query_rows = queries.reshape(rows, head_dim)

    with jax.named_scope("gather_queries"):
        copies = jnp.broadcast_to(query_rows[None], (ctx, rows, head_dim))
        visiting = lax.all_to_all(copies, CTX_ORDER, 0, 0, tiled=False)
    with jax.named_scope("swap_weight"):
        halves = out_weight.reshape(2, depth // 2, width)
        given = lax.dynamic_index_in_dim(halves, 1 - half, 0, keepdims=False)
        cut = depth // 8 * 3
        taken = [
            lax.ppermute(part, "zl", [(0, 1), (1, 0)]) for part in (given[:cut], given[cut:])
        ]
    with jax.named_scope("suffix_attention"):
        home_numer, home_stat = pl.pallas_call(
            functools.partial(suffix_kernel, conts=conts),
            in_specs=[SMEM, VMEM, VMEM, VMEM],
            out_specs=[VMEM, VMEM],
            out_shape=[
                jax.ShapeDtypeStruct((rows, head_dim), jnp.float32),
                jax.ShapeDtypeStruct((8, head_dim), jnp.float32),
            ],
            compiler_params=small,
            cost_estimate=pl.CostEstimate(
                flops=4 * conts * slots * head_dim * head_dim,
                bytes_accessed=4 * conts * slots * head_dim,
                transcendentals=conts * slots * head_dim,
            ),
        )(
            suffix_len,
            query_rows,
            suffix_keys.reshape(conts * slots, head_dim),
            suffix_values.reshape(conts * slots, head_dim),
        )
    visiting, home_numer, home_stat = lax.optimization_barrier(
        (visiting, home_numer, home_stat)
    )
    with jax.named_scope("prompt_attention"):
        sent = pl.pallas_call(
            prompt_kernel,
            in_specs=[VMEM, VMEM, HBM],
            out_specs=VMEM,
            scratch_shapes=[
                pltpu.VMEM((tokens, head_dim), jnp.bfloat16),
                pltpu.SemaphoreType.DMA,
            ],
            out_shape=jax.ShapeDtypeStruct((ctx, rows + STAT_ROWS, head_dim), jnp.bfloat16),
            compiler_params=large,
            cost_estimate=pl.CostEstimate(
                flops=4 * ctx * rows * tokens * head_dim,
                bytes_accessed=4 * tokens * head_dim,
                transcendentals=ctx * rows * tokens,
            ),
        )(
            visiting,
            prompt_keys.reshape(tokens, head_dim),
            pltpu.with_memory_space_constraint(
                prompt_values.reshape(tokens, head_dim), pltpu.HBM
            ),
        )
    sent, taken[0] = lax.optimization_barrier((sent, taken[0]))
    with jax.named_scope("return_partials"):
        back = lax.all_to_all(sent, CTX_ORDER, 0, 0, tiled=False)
    with jax.named_scope("combine"):
        attended, copies = pl.pallas_call(
            functools.partial(combine_kernel, sides=[home // rep % 2 for home in homes]),
            in_specs=[SMEM, VMEM, VMEM, VMEM],
            out_specs=[VMEM, VMEM],
            out_shape=[
                jax.ShapeDtypeStruct((rows, head_dim), jnp.bfloat16),
                jax.ShapeDtypeStruct((ctx * rep, rows // 2, head_dim), jnp.bfloat16),
            ],
            scratch_shapes=[pltpu.VMEM((head_dim, head_dim), jnp.float32)],
            compiler_params=small,
        )(lax.axis_index(CTX_ORDER[-1]).reshape(1), back, home_numer, home_stat)
    copies, taken[1] = lax.optimization_barrier((copies, taken[1]))
    with jax.named_scope("gather_attended"):
        everyone = lax.all_to_all(copies, ALL_ORDER, 0, 0, tiled=False)
    with jax.named_scope("project"):
        terms, attended = pl.pallas_call(
            functools.partial(project_kernel, homes=homes),
            in_specs=[SMEM] + [VMEM] * 5,
            out_specs=[VMEM, HBM],
            out_shape=[
                jax.ShapeDtypeStruct((2 * kvh, ctx * rep * conts // kvh, width), jnp.bfloat16),
                jax.ShapeDtypeStruct((rows, head_dim), jnp.bfloat16),
            ],
            scratch_shapes=[
                pltpu.VMEM((ctx * rep * rows // 2, head_dim), jnp.float32),
                pltpu.SemaphoreType.DMA,
            ],
            compiler_params=small,
        )(half.reshape(1), everyone, out_weight, taken[0], taken[1], attended)
    with jax.named_scope("sum_heads"):
        parts = lax.all_to_all(terms, KVH + ("zl",), 0, 0, tiled=False)
        projected = pl.pallas_call(
            sum_kernel,
            in_specs=[VMEM],
            out_specs=VMEM,
            out_shape=jax.ShapeDtypeStruct(parts.shape[1:], jnp.bfloat16),
            compiler_params=small,
        )(parts)
    return (attended.reshape(conts, heads, head_dim), projected)


def solution(mesh):
    ctx, kvh, rep = (mesh.shape[name] for name in ("ctx", "kvh", "rep"))
    fine = Mesh(
        mesh.devices.reshape(2, 2, ctx // 8, 2, kvh // 2, 2, 2, rep // 2),
        CTX + KVH + REP,
    )
    groups = CTX + REP
    in_specs = (
        P(groups, KVH, None),
        P(CTX, KVH, None),
        P(CTX, KVH, None),
        P(groups, None, KVH, None),
        P(groups, None, KVH, None),
        P(groups),
        P(KVH, groups),
    )
    out_specs = (P(groups, KVH, None), P(KVH, groups))
    return jax.shard_map(body, mesh=fine, in_specs=in_specs, out_specs=out_specs, check_vma=False)
```
